32 devices in a mesh: mix: 2 (over x), seq: 16 (over z, y, core).
Axes of the slice: x: 2, y: 2, z: 4, core: 2. Of those that a mesh axis runs over, the one named last changes fastest.
Arguments:
- frames: bfloat16 [4096, 1024], P(('mix', 'seq')), parts along dimension 0, may hold values from -18 to 18
- segment_ids: int32 [4096], P(('mix', 'seq')), parts along dimension 0, may hold values from 0 to 2, never falling along the last dimension, each value on 1 to 1500 neighbouring positions
- out_grad: bfloat16 [4096, 1024], P(('mix', 'seq')), parts along dimension 0, may hold values from -6 to 6
- ln_gain: float32 [2048], P(('mix', 'seq')), parts along dimension 0, may hold values from 0.5 to 2
- w_in: bfloat16 [2048, 2048], P(('mix', 'seq')), parts along dimension 0, may hold values from -0.1875 to 0.1875
- dw_kernel: float32 [62, 1024], P('mix', 'seq'), parts along dimension 0, may hold values from -1 to 1
- bn_gain: float32 [2048], P(('mix', 'seq')), parts along dimension 0, may hold values from 0.5 to 2
- bn_bias: float32 [2048], P(('mix', 'seq')), parts along dimension 0, may hold values from -3 to 3
- w_out: bfloat16 [2048, 1024], P(('mix', 'seq')), parts along dimension 0, may hold values from -0.1875 to 0.1875
Outputs:
- outputs: bfloat16 [4096, 1024], P(('mix', 'seq')), parts along dimension 0
- grad_frames: bfloat16 [4096, 1024], P(('mix', 'seq')), parts along dimension 0
- grad_w_in: float32 [2048, 2048], P(('mix', 'seq')), parts along dimension 0
- grad_w_out: float32 [2048, 1024], P(('mix', 'seq')), parts along dimension 0
- grad_kernel: float32 [62, 1024], P('mix', 'seq'), parts along dimension 0
- grad_ln_gain: float32 [2048], P(('mix', 'seq')), parts along dimension 0
- grad_bn_gain: float32 [2048], P(('mix', 'seq')), parts along dimension 0
- grad_bn_bias: float32 [2048], P(('mix', 'seq')), parts along dimension 0
The draws below stay inside these ranges and needn't reach their ends.
There are 2 independent parts, one for each index of `mix`. The reference program is written for one: setup_inputs(seed, part) draws one part's arguments, and reference() takes and returns one part's arrays. A program takes and returns all parts, laid end to end along the dimension named above; each array names one. Nothing has to cross between parts.
Inputs may be any that keep to these rules, and one draw needn't show every extreme that they name: `segment_ids`: ids never fall along the stream; every utterance number is used, by 1 to 1500 consecutive frames, one utterance exactly 1500.
All inputs are finite; a program needn't handle non-finite values.
Results may differ from the reference program's by a relative error of at most 0.012.
The reference program's roundings to bfloat16 on the way (of `ln_x`, `glu`, `activation` and `grad_hidden`) count: a program that leaves them out, or rounds other values in their place, can miss the bound.
Values may be sent and summed in bfloat16 or wider, within the bound.
A program may use at most 128 MiB of HBM per device.

```python
import math
import jax
import jax.numpy as jnp
import numpy as np
from jax import lax

D = 1024
KERNEL = 31
FRAMES = 2048
MAXLEN = 1500
UTTS = 3


def draw_frames(key, part):
    noise_key, pattern_key = jax.random.split(key)
    position = jnp.arange(FRAMES, dtype=jnp.float32)[:, None] / FRAMES
    noise = jax.random.truncated_normal(noise_key, -6.0, 6.0, (FRAMES, D), jnp.float32)
    pattern = jax.random.truncated_normal(pattern_key, -4.0, 4.0, (D,), jnp.float32)
    rising = 3.0 * position
    return (noise + rising * pattern).astype(jnp.bfloat16)


def shard_levels(key, extent, cuts, least, largest):
    factor_of, own = 1.0, jax.random.fold_in(key, 6)
    for axis_at, parts in cuts:
        steps = jnp.exp(jax.random.uniform(jax.random.fold_in(own, axis_at), (parts,), jnp.float32, least / len(cuts), largest / len(cuts)))
        factor_of = factor_of * jnp.repeat(steps, extent[axis_at] // parts).reshape([-1 if axis == axis_at else 1 for axis in range(len(extent))])
    return factor_of


def profile(amount, total, bound, lean):
    weights = [(1 << 20) // math.isqrt(rank ** lean) + 1 for rank in range(2, amount + 1)]
    surplus, counts = total - bound - (amount - 1), [1] * (amount - 1)
    while surplus > 0:
        candidates = [i for i in range(amount - 1) if counts[i] < bound]
        whole, remaining = sum([weights[i] for i in candidates]), surplus
        for i in candidates:
            addition = min(bound - counts[i], max(1, remaining * weights[i] // whole), surplus)
            counts[i] = counts[i] + addition
            surplus = surplus - addition
    return np.array([bound] + counts)


def ragged(own_key, amount, total, limit, skew):
    if amount == 2:
        one = jax.random.randint(own_key, (), max(1, total - limit), min(limit, total - 1) + 1)
        return jnp.stack([one, total - one])
    sizes = jnp.asarray(profile(amount, total, limit, skew), jnp.int32)
    pairs = (amount - 1) // 2
    giver, taker = sizes[1:1 + 2 * pairs:2], sizes[2:2 + 2 * pairs:2]
    slack = jnp.minimum(giver - 1, limit - taker)
    passed = jax.random.randint(jax.random.fold_in(own_key, 1), (pairs,), 0, 1 << 20) % (slack + 1)
    sizes = sizes.at[1:1 + 2 * pairs:2].set(giver - passed).at[2:2 + 2 * pairs:2].set(taker + passed)
    return sizes[jax.random.permutation(jax.random.fold_in(own_key, 2), amount)]


def normal_values(key, dims, deviation, limit, pieces=(), kind=jnp.bfloat16):
    result = deviation * jax.random.normal(key, dims, jnp.float32)
    if pieces:
        result = result * shard_levels(key, dims, pieces, -0.22, 0.18)
    return jnp.clip(result, -limit, limit).astype(kind)


def setup_inputs(seed: int = 0, part: int = 0) -> dict:
    arg_keys = jax.random.split(jax.random.key(seed), 10)
    part_keys = jax.random.split(jax.random.fold_in(arg_keys[9], part), 10)
    frames = draw_frames(jax.random.fold_in(jax.random.fold_in(arg_keys[9], part), 71), part)
    segment_ids = jnp.searchsorted(jnp.cumsum(ragged(part_keys[1], UTTS, FRAMES, MAXLEN, 2)), jnp.arange(FRAMES), side="right").astype(jnp.int32)
    out_grad = normal_values(part_keys[2], (FRAMES, D), 1.0, 6.0, ((0, 16),))
    ln_gain = jnp.clip(jnp.exp(math.log(2.0) - 1.3862944 * jax.random.uniform(part_keys[3], (D,), jnp.float32) ** shard_levels(part_keys[3], (D,), ((0, 16),), -0.2, 0.2)), 0.5, 2.0)
    w_in = normal_values(part_keys[4], (D, 2 * D), D ** -0.5, 0.1875, ((0, 16),))
    dw_kernel = normal_values(part_keys[5], (KERNEL, D), KERNEL ** -0.5, 1.0, ((1, 16),), jnp.float32)
    bn_gain = jnp.clip(jnp.exp(math.log(2.0) - 1.3862944 * jax.random.uniform(part_keys[6], (D,), jnp.float32) ** shard_levels(part_keys[6], (D,), ((0, 16),), -0.2, 0.2)), 0.5, 2.0)
    bn_bias = normal_values(part_keys[7], (D,), 0.5, 3.0, ((0, 16),), jnp.float32)
    w_out = normal_values(part_keys[8], (D, D), D ** -0.5, 0.1875, ((0, 16),))
    return {"frames": frames, "segment_ids": segment_ids, "out_grad": out_grad, "ln_gain": ln_gain, "w_in": w_in, "dw_kernel": dw_kernel, "bn_gain": bn_gain, "bn_bias": bn_bias, "w_out": w_out}


EPSILON = 1e-05

def reference(frames, segment_ids, out_grad, ln_gain, w_in, dw_kernel, bn_gain, bn_bias, w_out):
    margin = KERNEL // 2
    grad_scale = 1.0 / math.sqrt(FRAMES)
    frames_float = frames.astype(jnp.float32)
    mean_ln = lax.optimization_barrier(jnp.mean(frames_float, axis=1, keepdims=True))
    centred = frames_float - mean_ln
    rstd_ln = lax.rsqrt(lax.optimization_barrier(jnp.mean(centred * centred, axis=1, keepdims=True)) + EPSILON)
    ln_hat = centred * rstd_ln
    ln_x = (ln_hat * ln_gain).astype(jnp.bfloat16)
    hidden = jnp.dot(ln_x, w_in, preferred_element_type=jnp.float32)
    left_half = hidden[:, :D]
    right_gate = jax.nn.sigmoid(hidden[:, D:])
    glu = (left_half * right_gate).astype(jnp.bfloat16)
    own_ids = segment_ids + 1
    padded_ids = jnp.pad(own_ids, margin)
    masks = [(padded_ids[tap_index:tap_index + FRAMES] == own_ids).astype(jnp.float32)[:, None] for tap_index in range(KERNEL)]
    padded_glu = jnp.pad(glu, ((margin, margin), (0, 0)))
    conv_out = jnp.zeros((FRAMES, D), jnp.float32)
    for tap_index in range(KERNEL):
        conv_out = conv_out + dw_kernel[tap_index] * padded_glu[tap_index:tap_index + FRAMES].astype(jnp.float32) * masks[tap_index]
    bn_mean = lax.optimization_barrier(jnp.sum(conv_out, axis=0)) / FRAMES
    bn_var = lax.optimization_barrier(jnp.sum((conv_out - bn_mean) ** 2, axis=0)) / FRAMES
    bn_rstd = lax.rsqrt(bn_var + EPSILON)
    bn_hat = (conv_out - bn_mean) * bn_rstd
    zed = bn_hat * bn_gain + bn_bias
    zed_gate = jax.nn.sigmoid(zed)
    activation = (zed * zed_gate).astype(jnp.bfloat16)
    projected = jnp.dot(activation, w_out, preferred_element_type=jnp.float32)
    outputs = (frames_float + projected).astype(jnp.bfloat16)
    grad_w_out = jnp.dot(activation.T, out_grad, preferred_element_type=jnp.float32) * grad_scale
    grad_act = jnp.dot(out_grad, w_out.T, preferred_element_type=jnp.float32)
    grad_zed = grad_act * zed_gate * (1.0 + zed * (1.0 - zed_gate))
    bias_total = lax.optimization_barrier(jnp.sum(grad_zed, axis=0))
    gain_total = lax.optimization_barrier(jnp.sum(grad_zed * bn_hat, axis=0))
    grad_conv = bn_gain * bn_rstd * (grad_zed - bias_total / FRAMES - bn_hat * gain_total / FRAMES)
    kernel_rows = [lax.optimization_barrier(jnp.sum(grad_conv * padded_glu[tap_index:tap_index + FRAMES].astype(jnp.float32) * masks[tap_index], axis=0)) for tap_index in range(KERNEL)]
    grad_kernel = jnp.stack(kernel_rows) * grad_scale
    padded_conv = jnp.pad(grad_conv, ((margin, margin), (0, 0)))
    grad_glu = jnp.zeros((FRAMES, D), jnp.float32)
    for tap_index in range(KERNEL):
        mirror = 2 * margin - tap_index
        grad_glu = grad_glu + dw_kernel[tap_index] * padded_conv[mirror:mirror + FRAMES] * masks[mirror]
    grad_hidden = jnp.concatenate([grad_glu * right_gate, grad_glu * left_half * right_gate * (1.0 - right_gate)], axis=1).astype(jnp.bfloat16)
    grad_w_in = jnp.dot(ln_x.T, grad_hidden, preferred_element_type=jnp.float32) * grad_scale
    grad_ln = jnp.dot(grad_hidden, w_in.T, preferred_element_type=jnp.float32)
    grad_ln_gain = lax.optimization_barrier(jnp.sum(grad_ln * ln_hat, axis=0)) * grad_scale
    grad_hat = grad_ln * ln_gain
    grad_input = rstd_ln * (grad_hat - lax.optimization_barrier(jnp.mean(grad_hat, axis=1, keepdims=True)) - ln_hat * lax.optimization_barrier(jnp.mean(grad_hat * ln_hat, axis=1, keepdims=True)))
    grad_frames = (out_grad.astype(jnp.float32) + grad_input).astype(jnp.bfloat16)
    return (outputs, grad_frames, grad_w_in, grad_w_out, grad_kernel, grad_ln_gain, gain_total * grad_scale, bias_total * grad_scale)
```

```python
import math

import jax
import jax.numpy as jnp
from jax import lax
from jax.experimental import pallas as pl
from jax.experimental.pallas import tpu as pltpu
from jax.sharding import PartitionSpec as P

EPSILON = 1e-05


def with_halo(cells, sides, width):
    for axis, dim in sides:
        count = lax.axis_size(axis)
        ends = count - 1
        head = lax.slice_in_dim(cells, 0, width, axis=dim)
        tail = lax.slice_in_dim(cells, cells.shape[dim] - width, cells.shape[dim], axis=dim)
        cells = jnp.concatenate(
            [
                lax.ppermute(tail, axis, [(i, (i + 1) % count) for i in range(ends)]),
                cells,
                lax.ppermute(head, axis, [((i + 1) % count, i) for i in range(ends)]),
            ],
            axis=dim,
        )
    return cells


def local(frames, segment_ids, out_grad, ln_gain, w_in, dw_kernel, bn_gain, bn_bias, w_out):
    frame_count = frames.shape[0]
    width = frames.shape[1]
    taps = dw_kernel.shape[0]
    margin = taps // 2
    devices = lax.axis_size("seq")
    stream = frame_count * devices
    grad_scale = 1.0 / math.sqrt(stream)
    share = width // devices
    gains, kernel, bn_scale, bn_shift = (
        lax.all_gather(ln_gain, "seq", axis=0, tiled=True),
        lax.all_gather(dw_kernel, "seq", axis=1, tiled=True),
        lax.all_gather(bn_gain, "seq", axis=0, tiled=True),
        lax.all_gather(bn_bias, "seq", axis=0, tiled=True),
    )
    own_ids = segment_ids + 1
    padded_ids = with_halo(own_ids, (("seq", 0),), margin)
    masks = [
        (padded_ids[tap_index : tap_index + frame_count] == own_ids).astype(jnp.float32)[:, None]
        for tap_index in range(taps)
    ]
    frames_float = frames.astype(jnp.float32)
    mean_ln = jnp.mean(frames_float, axis=1, keepdims=True)
    centred = frames_float - mean_ln
    rstd_ln = lax.rsqrt(jnp.mean(centred * centred, axis=1, keepdims=True) + EPSILON)
    ln_hat = centred * rstd_ln
    ln_x = (ln_hat * gains).astype(jnp.bfloat16)
    columns = ln_x
    hidden = jnp.dot(
        columns, lax.all_gather(w_in, "seq", axis=0, tiled=True), preferred_element_type=jnp.float32
    )
    left_half = hidden[:, :width]
    right_gate = jax.nn.sigmoid(hidden[:, width:])
    glu = (left_half * right_gate).astype(jnp.bfloat16)
    padded_glu = with_halo(glu, (("seq", 0),), margin)
    conv_out = jnp.zeros((frame_count, width), jnp.float32)
    for tap_index in range(taps):
        conv_out = (
            conv_out
            + kernel[tap_index]
            * padded_glu[tap_index : tap_index + frame_count].astype(jnp.float32)
            * masks[tap_index]
        )
    plain_sums, square_sums = lax.psum(
        (jnp.sum(conv_out, axis=0), jnp.sum(conv_out * conv_out, axis=0)), "seq"
    )
    bn_mean = plain_sums / stream
    bn_var = square_sums / stream - bn_mean * bn_mean
    bn_rstd = lax.rsqrt(bn_var + EPSILON)
    bn_hat = (conv_out - bn_mean) * bn_rstd
    zed = bn_hat * bn_scale + bn_shift
    zed_gate = jax.nn.sigmoid(zed)
    activation = (zed * zed_gate).astype(jnp.bfloat16)
    columns = activation
    projected = jnp.dot(
        columns,
        lax.all_gather(w_out, "seq", axis=0, tiled=True),
        preferred_element_type=jnp.float32,
    )
    outputs = (frames_float + projected).astype(jnp.bfloat16)
    grad_w_out = lax.psum_scatter(
        jnp.einsum("fa,fb->ab", activation, out_grad, preferred_element_type=jnp.float32)
        * grad_scale,
        "seq",
        scatter_dimension=0,
        tiled=True,
    )
    grad_act = jnp.einsum(
        "fe,ne->fn",
        out_grad,
        lax.all_gather(w_out, "seq", axis=0, tiled=True),
        preferred_element_type=jnp.float32,
    )
    grad_zed = grad_act * zed_gate * (1.0 + zed * (1.0 - zed_gate))
    bias_total, gain_total = lax.psum(
        (jnp.sum(grad_zed, axis=0), jnp.sum(grad_zed * bn_hat, axis=0)), "seq"
    )
    grad_conv = bn_scale * bn_rstd * (grad_zed - bias_total / stream - bn_hat * gain_total / stream)
    first_channel = lax.axis_index("seq") * share
    grad_bn_bias = lax.dynamic_slice_in_dim(bias_total, first_channel, share, 0) * grad_scale
    grad_bn_gain = lax.dynamic_slice_in_dim(gain_total, first_channel, share, 0) * grad_scale
    kernel_rows = [
        jnp.sum(
            grad_conv
            * padded_glu[tap_index : tap_index + frame_count].astype(jnp.float32)
            * masks[tap_index],
            axis=0,
        )
        for tap_index in range(taps)
    ]
    kernel_term = jnp.stack(kernel_rows) * grad_scale
    padded_conv = with_halo(grad_conv, (("seq", 0),), margin)
    grad_glu = jnp.zeros((frame_count, width), jnp.float32)
    for tap_index in range(taps):
        mirror = 2 * margin - tap_index
        grad_glu = (
            grad_glu
            + kernel[tap_index] * padded_conv[mirror : mirror + frame_count] * masks[mirror]
        )
    grad_hidden = jnp.concatenate(
        [grad_glu * right_gate, grad_glu * left_half * right_gate * (1.0 - right_gate)], axis=1
    ).astype(jnp.bfloat16)
    grad_ln = jnp.einsum(
        "fe,ne->fn",
        grad_hidden,
        lax.all_gather(w_in, "seq", axis=0, tiled=True),
        preferred_element_type=jnp.float32,
    )
    in_term = (
        jnp.einsum("fa,fb->ab", ln_x, grad_hidden, preferred_element_type=jnp.float32) * grad_scale
    )
    gain_term = jnp.sum(grad_ln * ln_hat, axis=0) * grad_scale
    grad_w_in, grad_kernel, grad_ln_gain = (
        lax.psum_scatter(in_term, "seq", scatter_dimension=0, tiled=True),
        lax.psum_scatter(kernel_term, "seq", scatter_dimension=1, tiled=True),
        lax.psum_scatter(gain_term, "seq", scatter_dimension=0, tiled=True),
    )
    grad_hat = grad_ln * gains
    grad_input = rstd_ln * (
        grad_hat
        - jnp.mean(grad_hat, axis=1, keepdims=True)
        - ln_hat * jnp.mean(grad_hat * ln_hat, axis=1, keepdims=True)
    )
    grad_frames = (out_grad.astype(jnp.float32) + grad_input).astype(jnp.bfloat16)
    return (
        outputs,
        grad_frames,
        grad_w_in,
        grad_w_out,
        grad_kernel,
        grad_ln_gain,
        grad_bn_gain,
        grad_bn_bias,
    )


TEAM = 4
LINE = 4
PAD = 16
ROWS = 64
(
    S_WIN,
    S_GAIN,
    S_FRAMES,
    S_IDS,
    S_OG,
    S_WIN_Z,
    S_GAIN_Z,
    S_PRM,
    S_WOUT,
    S_IDS_HALO,
    S_GLU_HALO,
    S_BN,
    S_BN_BACK,
    S_GC_HALO,
    S_PROJ,
    S_GWOUT,
    S_GK,
    S_GWIN,
    S_GGAIN,
    S_GLN,
    S_GWIN_T,
    S_GGAIN_T,
    STAGES,
) = range(23)
F32 = jnp.float32
BF16 = jnp.bfloat16


def fused_kernel(
    frames_in,
    ids_in,
    og_in,
    gain_in,
    win_in,
    prm_in,
    wout_in,
    out_ref,
    gframes_ref,
    gwin_ref,
    gwout_ref,
    gk_ref,
    ggain_ref,
    gbn_ref,
    fr,
    idx,
    og,
    gains,
    gvec,
    win,
    prm,
    prml,
    wout,
    lnhat,
    rstd,
    lnx,
    left,
    gate,
    gext,
    conv,
    gact,
    act,
    bst,
    bst2,
    gcext,
    gh,
    gkacc,
    gkr,
    gkrecv,
    projs,
    projr,
    gwos,
    gwor,
    gwis,
    gwir,
    gwit,
    gwitr,
    glns,
    glnr,
    ggs,
    ggr,
    ggt,
    ggtr,
    send_sem,
    recv_sem,
):
    block, width = frames_in.shape
    group = block * TEAM
    chan = width // TEAM
    share = wout_in.shape[0]
    stream = group * LINE
    scale = 1.0 / math.sqrt(stream)
    me = lax.axis_index("seq")
    z, g = me // TEAM, me % TEAM

    def team(d):
        return z * TEAM + (g + d) % TEAM

    def line(d):
        return ((z + d) % LINE) * TEAM + g

    def rows(i, n):
        return pl.ds(pl.multiple_of(i * n, n), n)

    started = []

    def send(stage, d, source, target, device):
        copy = pltpu.make_async_remote_copy(
            src_ref=source,
            dst_ref=target,
            send_sem=send_sem.at[stage, d],
            recv_sem=recv_sem.at[stage, d],
            device_id={"seq": device},
            device_id_type=pl.DeviceIdType.MESH,
        )
        copy.start()
        started.append(copy)
        return copy

    def arrive(copies):
        for copy in copies:
            copy.wait_recv()

    order = (2, 1, 3)
    barrier = pltpu.get_barrier_semaphore()
    for d in (1, 2, 3):
        for device in (team(d), line(d)):
            pl.semaphore_signal(
                barrier, inc=1, device_id={"seq": device}, device_id_type=pl.DeviceIdType.MESH
            )
    pl.semaphore_wait(barrier, 6)

    c_win = [
        send(S_WIN, d, win_in.at[(g + d) % TEAM], win.at[rows(me, share)], team(d)) for d in order
    ]
    c_gain = [send(S_GAIN, d, gain_in, gains.at[me], team(d)) for d in order]
    c_prm = [send(S_PRM, d, prm_in, prm.at[z], line(d)) for d in order]
    c_frames = [send(S_FRAMES, d, frames_in, fr.at[rows(g, block)], team(d)) for d in order]
    ids_own = pl.ds(pl.multiple_of(PAD + g * block, PAD), block)
    c_ids = [send(S_IDS, d, ids_in, idx.at[ids_own], team(d)) for d in order]
    c_og = [send(S_OG, d, og_in, og.at[rows(g, block)], team(d)) for d in order]
    win[rows(me, share)] = win_in[g]
    gains[me] = gain_in[...]
    prm[z] = prm_in[...]
    fr[rows(g, block)] = frames_in[...]
    idx[ids_own] = ids_in[...]
    og[rows(g, block)] = og_in[...]
    wout[rows(z, share)] = wout_in[...]

    arrive(c_win)
    win_own = rows(z, share * TEAM)
    c_win_z = [send(S_WIN_Z, d, win.at[win_own], win.at[win_own], line(d)) for d in order]
    arrive(c_gain)
    team_own = pl.ds(z * TEAM, TEAM)
    c_gain_z = [send(S_GAIN_Z, d, gains.at[team_own], gains.at[team_own], line(d)) for d in order]
    c_wout = [send(S_WOUT, d, wout_in, wout.at[rows(z, share)], line(d)) for d in order]
    arrive(c_ids)
    c_idh = [
        send(S_IDS_HALO, 1, idx.at[pl.ds(group, PAD)], idx.at[pl.ds(0, PAD)], line(1)),
        send(S_IDS_HALO, 3, idx.at[pl.ds(PAD, PAD)], idx.at[pl.ds(PAD + group, PAD)], line(3)),
    ]

    arrive(c_gain_z)
    for j in range(width // 128):
        gvec[:, pl.ds(128 * j, 128)] = gains[2 * j] + gains[2 * j + 1]
    arrive(c_frames)

    @pl.loop(0, group // 32)
    def _(i):
        at = rows(i, 32)
        x = fr[at].astype(F32)
        centred = x - jnp.mean(x, axis=1, keepdims=True)
        r = lax.rsqrt(jnp.mean(centred * centred, axis=1, keepdims=True) + EPSILON)
        hat = centred * r
        lnhat[at] = hat
        rstd[at] = jnp.broadcast_to(r, (32, 128))
        lnx[at] = (hat * gvec[0:1, :]).astype(BF16)

    arrive(c_prm)
    prml[:, 0:128] = prm[0] + prm[1]
    prml[:, 128:256] = prm[2] + prm[3]
    arrive(c_idh)

    @pl.when(z == 0)
    def _():
        idx[pl.ds(0, PAD)] = jnp.full((PAD, 128), -1.0, F32)

    @pl.when(z == LINE - 1)
    def _():
        idx[pl.ds(PAD + group, PAD)] = jnp.full((PAD, 128), -1.0, F32)

    arrive(c_win_z)

    @pl.loop(0, TEAM)
    def _(i):
        at = rows(i, block)
        h = jnp.dot(lnx[at], win[...], preferred_element_type=F32)
        lh = h[:, :chan]
        rg = jax.nn.sigmoid(h[:, chan:])
        left[at] = lh
        gate[at] = rg
        value = (lh * rg).astype(BF16).astype(F32)
        inner = pl.ds(pl.multiple_of(PAD + i * block, PAD), block)
        gext[0, inner] = value[:, :128]
        gext[1, inner] = value[:, 128:]

    def halo(stage, ext):
        return [
            send(
                stage, 1, ext.at[:, pl.ds(group, PAD)], ext.at[:, pl.ds(0, PAD)], line(1)
            ),
            send(
                stage, 3, ext.at[:, pl.ds(PAD, PAD)], ext.at[:, pl.ds(PAD + group, PAD)], line(3)
            ),
        ]

    c_gh = halo(S_GLU_HALO, gext)
    chunks = group // ROWS

    def forward(c):
        at = rows(c, ROWS)
        own = idx[pl.ds(pl.multiple_of(PAD + c * ROWS, 8), ROWS)]
        total = [jnp.zeros((ROWS, 128), F32) for _ in range(2)]
        for k in range(31):
            there = pl.ds(c * ROWS + 1 + k, ROWS)
            same = idx[there] == own
            for t in range(2):
                term = jnp.where(same, gext[t, there], 0.0)
                total[t] = total[t] + prml[k : k + 1, 128 * t : 128 * t + 128] * term
        for t in range(2):
            conv[at, 128 * t : 128 * t + 128] = total[t]

    @pl.loop(1, chunks - 1)
    def _(c):
        forward(c)

    arrive(c_gh)

    @pl.loop(0, 2)
    def _(c):
        forward(c * (chunks - 1))

    part_mean = jnp.sum(conv[...], axis=0, keepdims=True) / group
    off = conv[...] - part_mean
    bst[0, 0] = jnp.broadcast_to(part_mean, (8, chan))
    bst[0, 1] = jnp.broadcast_to(jnp.sum(off * off, axis=0, keepdims=True), (8, chan))
    c_bn = [send(S_BN, d, bst.at[0], bst.at[d], line(d)) for d in order]

    arrive(c_wout)
    arrive(c_og)

    @pl.loop(0, TEAM)
    def _(i):
        at = rows(i, block)
        gact[at] = lax.dot_general(
            og[at], wout[...], (((1,), (1,)), ((), ())), preferred_element_type=F32
        )

    arrive(c_bn)
    means = [bst[d, 0] for d in range(LINE)]
    bn_mean8 = (means[0] + means[1] + means[2] + means[3]) / LINE
    spread = jnp.zeros((8, chan), F32)
    for d in range(LINE):
        shift = means[d] - bn_mean8
        spread = spread + bst[d, 1] + group * (shift * shift)
    bn_rstd = lax.rsqrt(spread / stream + EPSILON)[0:1]
    bn_mean = bn_mean8[0:1]
    bn_gain = prml[31:32, :]
    bn_bias = prml[32:33, :]

    def activate(i, sums):
        at = rows(i, ROWS)
        hat = (conv[at] - bn_mean) * bn_rstd
        zed = hat * bn_gain + bn_bias
        zg = jax.nn.sigmoid(zed)
        act[at] = (zed * zg).astype(BF16)
        gz = gact[at] * zg * (1.0 + zed * (1.0 - zg))
        conv[at] = hat
        gact[at] = gz
        fold = lambda v: jnp.sum(v.reshape(ROWS // 8, 8, chan), axis=0)
        return sums[0] + fold(gz), sums[1] + fold(gz * hat)

    zero = jnp.zeros((8, chan), F32)
    sums = lax.fori_loop(0, chunks, activate, (zero, zero))
    for j in range(2):
        bst2[0, j] = jnp.broadcast_to(jnp.sum(sums[j], axis=0, keepdims=True), (8, chan))
    c_bn2 = [send(S_BN_BACK, d, bst2.at[0], bst2.at[d], line(d)) for d in order]

    arrive(c_bn2)
    bias_total = (bst2[0, 0] + bst2[1, 0] + bst2[2, 0] + bst2[3, 0])[0:1]
    gain_total = (bst2[0, 1] + bst2[1, 1] + bst2[2, 1] + bst2[3, 1])[0:1]
    gbn_ref[0] = jnp.broadcast_to(gain_total * scale, (8, chan))
    gbn_ref[1] = jnp.broadcast_to(bias_total * scale, (8, chan))
    lead = bn_gain * bn_rstd
    bias_mean = bias_total / stream
    gain_mean = gain_total / stream

    @pl.loop(0, chunks)
    def _(i):
        at = rows(i, ROWS)
        inner = pl.ds(pl.multiple_of(PAD + i * ROWS, PAD), ROWS)
        gc = lead * (gact[at] - bias_mean - conv[at] * gain_mean)
        gcext[0, inner] = gc[:, :128]
        gcext[1, inner] = gc[:, 128:]

    c_gc = halo(S_GC_HALO, gcext)

    @pl.loop(0, TEAM)
    def _(i):
        at = rows(i, block)
        projs[i] = jnp.dot(act[at], wout[...], preferred_element_type=F32).astype(BF16)

    c_proj = [send(S_PROJ, d, projs.at[(g + d) % TEAM], projr.at[d], team(d)) for d in order]
    gwo = lax.dot_general(
        act[...], og[...], (((0,), (0,)), ((), ())), preferred_element_type=F32
    ).astype(BF16)
    for j in range(LINE):
        gwos[j] = gwo[j * share : (j + 1) * share]
    c_gwo = [send(S_GWOUT, d, gwos.at[(z + d) % LINE], gwor.at[d], line(d)) for d in order]

    gkacc[...] = jnp.zeros_like(gkacc)

    def backward(c):
        at = rows(c, ROWS)
        inner = pl.ds(pl.multiple_of(PAD + c * ROWS, 8), ROWS)
        own = idx[inner]
        value = [gext[t, inner] for t in range(2)]
        total = [jnp.zeros((ROWS, 128), F32) for _ in range(2)]
        for j in range(31):
            k = 30 - j
            there = pl.ds(c * ROWS + 1 + j, ROWS)
            same = idx[there] == own
            for t in range(2):
                lanes = slice(128 * t, 128 * t + 128)
                term = jnp.where(same, gcext[t, there], 0.0)
                total[t] = total[t] + prml[k : k + 1, lanes] * term
                fold = jnp.sum((value[t] * term).reshape(ROWS // 8, 8, 128), axis=0)
                gkacc[k, :, lanes] = gkacc[k, :, lanes] + fold
        for t in range(2):
            lanes = slice(128 * t, 128 * t + 128)
            rg = gate[at, lanes]
            first = total[t] * rg
            gh[at, lanes] = first.astype(BF16)
            gh[at, slice(chan + 128 * t, chan + 128 * t + 128)] = (
                total[t] * left[at, lanes] * rg * (1.0 - rg)
            ).astype(BF16)

    @pl.loop(1, chunks - 1)
    def _(c):
        backward(c)

    arrive(c_gc)

    @pl.loop(0, 2)
    def _(c):
        backward(c * (chunks - 1))

    for d in (2, 1, 3, 0):
        to = (z + d) % LINE
        gwis[d] = lax.dot_general(
            lnx[:, rows(to, chan)], gh[...], (((0,), (0,)), ((), ())), preferred_element_type=F32
        ).astype(BF16)
        if d:
            started_copy = send(S_GWIN, d, gwis.at[d], gwir.at[d], line(d))
            c_gwi = [started_copy] if d == 2 else c_gwi + [started_copy]

    for t in range(2):
        gkr[t] = jnp.sum(gkacc[:, :, 128 * t : 128 * t + 128], axis=1)
    c_gk = [send(S_GK, d, gkr.at[((z + d) % LINE) // 2], gkrecv.at[d], line(d)) for d in order]

    def lower(i, total):
        at = rows(i, block)
        part = lax.dot_general(
            gh[at], win[...], (((1,), (1,)), ((), ())), preferred_element_type=F32
        )
        glns[i] = part.astype(BF16)
        return total + jnp.sum(part * lnhat[at], axis=0, keepdims=True)

    gg = lax.fori_loop(0, TEAM, lower, jnp.zeros((1, width), F32))
    c_gln = [send(S_GLN, d, glns.at[(g + d) % TEAM], glnr.at[d], team(d)) for d in order]
    for j in range(LINE):
        ggs[j] = jnp.broadcast_to(gg[:, j * chan : (j + 1) * chan], (8, chan))
    c_gg = [send(S_GGAIN, d, ggs.at[(z + d) % LINE], ggr.at[d], line(d)) for d in order]

    arrive(c_proj)
    o = frames_in[...].astype(F32) + projs[g].astype(F32)
    for d in (1, 2, 3):
        o = o + projr[d].astype(F32)
    out_ref[...] = o.astype(BF16)
    arrive(c_gwo)
    o = gwos[z].astype(F32)
    for d in (1, 2, 3):
        o = o + gwor[d].astype(F32)
    gwout_ref[...] = o * scale
    arrive(c_gk)
    gk_ref[...] = (gkr[z // 2] + gkrecv[1] + gkrecv[2] + gkrecv[3]) * scale

    arrive(c_gg)
    gs = ggs[z] + ggr[1] + ggr[2] + ggr[3]
    ggt[0] = gs[:, :128]
    ggt[1] = gs[:, 128:]
    c_ggt = [send(S_GGAIN_T, d, ggt.at[((g + d) % TEAM) // 2], ggtr.at[d], team(d)) for d in order]

    arrive(c_gln)

    @pl.loop(0, block // 32)
    def _(i):
        at = rows(i, 32)
        there = pl.ds(pl.multiple_of(g * block + i * 32, 32), 32)
        gl = glns[g, at].astype(F32)
        for d in (1, 2, 3):
            gl = gl + glnr[d, at].astype(F32)
        hat = lnhat[there]
        ghat = gl * gvec[0:1, :]
        gx = rstd[there][:, 0:1] * (
            ghat
            - jnp.mean(ghat, axis=1, keepdims=True)
            - hat * jnp.mean(ghat * hat, axis=1, keepdims=True)
        )
        gframes_ref[at] = (og_in[at].astype(F32) + gx).astype(BF16)

    arrive(c_gwi)
    o = gwis[0].astype(F32)
    for d in (1, 2, 3):
        o = o + gwir[d].astype(F32)
    o = o.astype(BF16)
    for j in range(TEAM):
        gwit[j] = o[j * share : (j + 1) * share]
    c_gwt = [send(S_GWIN_T, d, gwit.at[(g + d) % TEAM], gwitr.at[d], team(d)) for d in order]
    arrive(c_ggt)
    ggain_ref[...] = (ggt[g // 2] + ggtr[1] + ggtr[2] + ggtr[3]) * scale
    gwin_ref[g] = gwit[g].astype(F32) * scale
    arrive(c_gwt)
    for d in (1, 2, 3):
        gwin_ref[(g + TEAM - d) % TEAM] = gwitr[d].astype(F32) * scale
    for copy in started:
        copy.wait_send()


def fused(frames, segment_ids, out_grad, ln_gain, w_in, dw_kernel, bn_gain, bn_bias, w_out):
    block, width = frames.shape
    share = w_in.shape[0]
    group = block * TEAM
    chan = width // TEAM
    me = lax.axis_index("seq")
    z, g = me // TEAM, me % TEAM
    ids = jnp.broadcast_to(segment_ids.astype(F32)[:, None], (block, 128))
    lane_half = jnp.arange(128) // share

    def halves(rows_, odd):
        both = jnp.concatenate([rows_, rows_], axis=1)
        return jnp.where(lane_half[None, :] == odd, both, 0.0)

    gain = halves(jnp.broadcast_to(ln_gain[None, :], (8, share)), g % 2)
    prm = halves(
        jnp.concatenate(
            [dw_kernel, bn_gain[None], bn_bias[None], jnp.zeros((7, share), F32)], axis=0
        ),
        z % 2,
    )
    win = (
        w_in.reshape(share, 2, LINE, TEAM, share)
        .transpose(3, 0, 1, 2, 4)
        .reshape(TEAM, share, 2 * chan)
    )
    vmem = pl.BlockSpec(memory_space=pltpu.VMEM)
    shape = jax.ShapeDtypeStruct
    ext = group + 2 * PAD
    out, gframes, gwin, gwout, gk, ggain, gbn = pl.pallas_call(
        fused_kernel,
        out_shape=[
            shape((block, width), BF16),
            shape((block, width), BF16),
            shape((TEAM, share, 2 * chan), F32),
            shape((share, width), F32),
            shape((32, 128), F32),
            shape((8, 128), F32),
            shape((2, 8, chan), F32),
        ],
        in_specs=[vmem] * 7,
        out_specs=[vmem] * 7,
        scratch_shapes=[
            pltpu.VMEM((group, width), BF16),
            pltpu.VMEM((ext, 128), F32),
            pltpu.VMEM((group, width), BF16),
            pltpu.VMEM((TEAM * LINE, 8, 128), F32),
            pltpu.VMEM((8, width), F32),
            pltpu.VMEM((width, 2 * chan), BF16),
            pltpu.VMEM((LINE, 40, 128), F32),
            pltpu.VMEM((40, chan), F32),
            pltpu.VMEM((chan, width), BF16),
            pltpu.VMEM((group, width), F32),
            pltpu.VMEM((group, 128), F32),
            pltpu.VMEM((group, width), BF16),
            pltpu.VMEM((group, chan), F32),
            pltpu.VMEM((group, chan), F32),
            pltpu.VMEM((2, ext, 128), F32),
            pltpu.VMEM((group, chan), F32),
            pltpu.VMEM((group, chan), F32),
            pltpu.VMEM((group, chan), BF16),
            pltpu.VMEM((LINE, 2, 8, chan), F32),
            pltpu.VMEM((LINE, 2, 8, chan), F32),
            pltpu.VMEM((2, ext, 128), F32),
            pltpu.VMEM((group, 2 * chan), BF16),
            pltpu.VMEM((32, 8, chan), F32),
            pltpu.VMEM((2, 32, 128), F32),
            pltpu.VMEM((LINE, 32, 128), F32),
            pltpu.VMEM((TEAM, block, width), BF16),
            pltpu.VMEM((TEAM, block, width), BF16),
            pltpu.VMEM((LINE, share, width), BF16),
            pltpu.VMEM((LINE, share, width), BF16),
            pltpu.VMEM((LINE, chan, 2 * chan), BF16),
            pltpu.VMEM((LINE, chan, 2 * chan), BF16),
            pltpu.VMEM((TEAM, share, 2 * chan), BF16),
            pltpu.VMEM((TEAM, share, 2 * chan), BF16),
            pltpu.VMEM((TEAM, block, width), BF16),
            pltpu.VMEM((TEAM, block, width), BF16),
            pltpu.VMEM((LINE, 8, chan), F32),
            pltpu.VMEM((LINE, 8, chan), F32),
            pltpu.VMEM((2, 8, 128), F32),
            pltpu.VMEM((TEAM, 8, 128), F32),
            pltpu.SemaphoreType.DMA((STAGES, 4)),
            pltpu.SemaphoreType.DMA((STAGES, 4)),
        ],
        compiler_params=pltpu.CompilerParams(
            collective_id=0, has_side_effects=True, vmem_limit_bytes=48 * 1024 * 1024
        ),
    )(frames, ids, out_grad, gain, win, prm, w_out)
    gwin = (
        gwin.reshape(TEAM, share, 2, LINE, share)
        .transpose(1, 2, 3, 0, 4)
        .reshape(share, 2 * width)
    )
    gk = jnp.where(z % 2 == 0, gk[:31, :share], gk[:31, share:])
    ggain = jnp.where(g % 2 == 0, ggain[0, :share], ggain[0, share:])
    gbn = lax.dynamic_slice_in_dim(gbn[:, 0, :], z * share, share, 1)
    return out, gframes, gwin, gwout, gk, ggain, gbn[0], gbn[1]


def solution(mesh):
    small = mesh.shape["seq"] == TEAM * LINE
    return jax.shard_map(
        fused if small else local,
        mesh=mesh,
        in_specs=(
            P(("mix", "seq"), None),
            P(("mix", "seq")),
            P(("mix", "seq"), None),
            P(("mix", "seq")),
            P(("mix", "seq"), None),
            P("mix", "seq"),
            P(("mix", "seq")),
            P(("mix", "seq")),
            P(("mix", "seq"), None),
        ),
        out_specs=(
            P(("mix", "seq"), None),
            P(("mix", "seq"), None),
            P(("mix", "seq"), None),
            P(("mix", "seq"), None),
            P("mix", "seq"),
            P(("mix", "seq")),
            P(("mix", "seq")),
            P(("mix", "seq")),
        ),
        check_vma=False,
    )
```

```python
import math

import jax
import jax.numpy as jnp
from jax import lax
from jax.experimental import pallas as pl
from jax.experimental.pallas import tpu as pltpu
from jax.sharding import PartitionSpec as P

EPSILON = 1e-05


def with_halo(cells, sides, width):
    for axis, dim in sides:
        count = lax.axis_size(axis)
        ends = count - 1
        head = lax.slice_in_dim(cells, 0, width, axis=dim)
        tail = lax.slice_in_dim(cells, cells.shape[dim] - width, cells.shape[dim], axis=dim)
        cells = jnp.concatenate(
            [
                lax.ppermute(tail, axis, [(i, (i + 1) % count) for i in range(ends)]),
                cells,
                lax.ppermute(head, axis, [((i + 1) % count, i) for i in range(ends)]),
            ],
            axis=dim,
        )
    return cells


def local(frames, segment_ids, out_grad, ln_gain, w_in, dw_kernel, bn_gain, bn_bias, w_out):
    frame_count = frames.shape[0]
    width = frames.shape[1]
    taps = dw_kernel.shape[0]
    margin = taps // 2
    devices = lax.axis_size("seq")
    stream = frame_count * devices
    grad_scale = 1.0 / math.sqrt(stream)
    share = width // devices
    gains, kernel, bn_scale, bn_shift = (
        lax.all_gather(ln_gain, "seq", axis=0, tiled=True),
        lax.all_gather(dw_kernel, "seq", axis=1, tiled=True),
        lax.all_gather(bn_gain, "seq", axis=0, tiled=True),
        lax.all_gather(bn_bias, "seq", axis=0, tiled=True),
    )
    own_ids = segment_ids + 1
    padded_ids = with_halo(own_ids, (("seq", 0),), margin)
    masks = [
        (padded_ids[tap_index : tap_index + frame_count] == own_ids).astype(jnp.float32)[:, None]
        for tap_index in range(taps)
    ]
    frames_float = frames.astype(jnp.float32)
    mean_ln = jnp.mean(frames_float, axis=1, keepdims=True)
    centred = frames_float - mean_ln
    rstd_ln = lax.rsqrt(jnp.mean(centred * centred, axis=1, keepdims=True) + EPSILON)
    ln_hat = centred * rstd_ln
    ln_x = (ln_hat * gains).astype(jnp.bfloat16)
    columns = ln_x
    hidden = jnp.dot(
        columns, lax.all_gather(w_in, "seq", axis=0, tiled=True), preferred_element_type=jnp.float32
    )
    left_half = hidden[:, :width]
    right_gate = jax.nn.sigmoid(hidden[:, width:])
    glu = (left_half * right_gate).astype(jnp.bfloat16)
    padded_glu = with_halo(glu, (("seq", 0),), margin)
    conv_out = jnp.zeros((frame_count, width), jnp.float32)
    for tap_index in range(taps):
        conv_out = (
            conv_out
            + kernel[tap_index]
            * padded_glu[tap_index : tap_index + frame_count].astype(jnp.float32)
            * masks[tap_index]
        )
    plain_sums, square_sums = lax.psum(
        (jnp.sum(conv_out, axis=0), jnp.sum(conv_out * conv_out, axis=0)), "seq"
    )
    bn_mean = plain_sums / stream
    bn_var = square_sums / stream - bn_mean * bn_mean
    bn_rstd = lax.rsqrt(bn_var + EPSILON)
    bn_hat = (conv_out - bn_mean) * bn_rstd
    zed = bn_hat * bn_scale + bn_shift
    zed_gate = jax.nn.sigmoid(zed)
    activation = (zed * zed_gate).astype(jnp.bfloat16)
    columns = activation
    projected = jnp.dot(
        columns,
        lax.all_gather(w_out, "seq", axis=0, tiled=True),
        preferred_element_type=jnp.float32,
    )
    outputs = (frames_float + projected).astype(jnp.bfloat16)
    grad_w_out = lax.psum_scatter(
        jnp.einsum("fa,fb->ab", activation, out_grad, preferred_element_type=jnp.float32)
        * grad_scale,
        "seq",
        scatter_dimension=0,
        tiled=True,
    )
    grad_act = jnp.einsum(
        "fe,ne->fn",
        out_grad,
        lax.all_gather(w_out, "seq", axis=0, tiled=True),
        preferred_element_type=jnp.float32,
    )
    grad_zed = grad_act * zed_gate * (1.0 + zed * (1.0 - zed_gate))
    bias_total, gain_total = lax.psum(
        (jnp.sum(grad_zed, axis=0), jnp.sum(grad_zed * bn_hat, axis=0)), "seq"
    )
    grad_conv = bn_scale * bn_rstd * (grad_zed - bias_total / stream - bn_hat * gain_total / stream)
    first_channel = lax.axis_index("seq") * share
    grad_bn_bias = lax.dynamic_slice_in_dim(bias_total, first_channel, share, 0) * grad_scale
    grad_bn_gain = lax.dynamic_slice_in_dim(gain_total, first_channel, share, 0) * grad_scale
    kernel_rows = [
        jnp.sum(
            grad_conv
            * padded_glu[tap_index : tap_index + frame_count].astype(jnp.float32)
            * masks[tap_index],
            axis=0,
        )
        for tap_index in range(taps)
    ]
    kernel_term = jnp.stack(kernel_rows) * grad_scale
    padded_conv = with_halo(grad_conv, (("seq", 0),), margin)
    grad_glu = jnp.zeros((frame_count, width), jnp.float32)
    for tap_index in range(taps):
        mirror = 2 * margin - tap_index
        grad_glu = (
            grad_glu
            + kernel[tap_index] * padded_conv[mirror : mirror + frame_count] * masks[mirror]
        )
    grad_hidden = jnp.concatenate(
        [grad_glu * right_gate, grad_glu * left_half * right_gate * (1.0 - right_gate)], axis=1
    ).astype(jnp.bfloat16)
    grad_ln = jnp.einsum(
        "fe,ne->fn",
        grad_hidden,
        lax.all_gather(w_in, "seq", axis=0, tiled=True),
        preferred_element_type=jnp.float32,
    )
    in_term = (
        jnp.einsum("fa,fb->ab", ln_x, grad_hidden, preferred_element_type=jnp.float32) * grad_scale
    )
    gain_term = jnp.sum(grad_ln * ln_hat, axis=0) * grad_scale
    grad_w_in, grad_kernel, grad_ln_gain = (
        lax.psum_scatter(in_term, "seq", scatter_dimension=0, tiled=True),
        lax.psum_scatter(kernel_term, "seq", scatter_dimension=1, tiled=True),
        lax.psum_scatter(gain_term, "seq", scatter_dimension=0, tiled=True),
    )
    grad_hat = grad_ln * gains
    grad_input = rstd_ln * (
        grad_hat
        - jnp.mean(grad_hat, axis=1, keepdims=True)
        - ln_hat * jnp.mean(grad_hat * ln_hat, axis=1, keepdims=True)
    )
    grad_frames = (out_grad.astype(jnp.float32) + grad_input).astype(jnp.bfloat16)
    return (
        outputs,
        grad_frames,
        grad_w_in,
        grad_w_out,
        grad_kernel,
        grad_ln_gain,
        grad_bn_gain,
        grad_bn_bias,
    )


TEAM = 4
LINE = 4
PAD = 16
ROWS = 64
(
    S_WIN,
    S_GAIN,
    S_FRAMES,
    S_IDS,
    S_OG,
    S_WIN_Z,
    S_GAIN_Z,
    S_PRM,
    S_WOUT,
    S_IDS_HALO,
    S_GLU_HALO,
    S_BN,
    S_BN_BACK,
    S_GC_HALO,
    S_PROJ,
    S_GWOUT,
    S_GK,
    S_GWIN,
    S_GGAIN,
    S_GLN,
    S_GWIN_T,
    S_GGAIN_T,
    S_GWIN_B,
    S_GWIN_TB,
    STAGES,
) = range(25)
F32 = jnp.float32
BF16 = jnp.bfloat16


def fused_kernel(
    frames_in,
    ids_in,
    og_in,
    gain_in,
    win_in,
    prm_in,
    wout_in,
    out_ref,
    gframes_ref,
    gwin_ref,
    gwout_ref,
    gk_ref,
    ggain_ref,
    gbn_ref,
    fr,
    idx,
    og,
    gains,
    gvec,
    win,
    prm,
    prml,
    wout,
    lnhat,
    rstd,
    lnx,
    left,
    gate,
    gext,
    conv,
    gact,
    act,
    bst,
    bst2,
    gcext,
    gh,
    hs,
    hr,
    gkacc,
    gkr,
    gkrecv,
    projs,
    projr,
    gwos,
    gwor,
    gwis,
    gwir,
    gwit,
    gwitr,
    glns,
    glnr,
    ggs,
    ggr,
    ggt,
    ggtr,
    send_sem,
    recv_sem,
):
    block, width = frames_in.shape
    group = block * TEAM
    chan = width // TEAM
    share = wout_in.shape[0]
    stream = group * LINE
    scale = 1.0 / math.sqrt(stream)
    me = lax.axis_index("seq")
    z, g = me // TEAM, me % TEAM

    def team(d):
        return z * TEAM + (g + d) % TEAM

    def line(d):
        return ((z + d) % LINE) * TEAM + g

    def rows(i, n):
        return pl.ds(pl.multiple_of(i * n, n), n)

    started = []

    def send(stage, d, source, target, device):
        copy = pltpu.make_async_remote_copy(
            src_ref=source,
            dst_ref=target,
            send_sem=send_sem.at[stage, d],
            recv_sem=recv_sem.at[stage, d],
            device_id={"seq": device},
            device_id_type=pl.DeviceIdType.MESH,
        )
        copy.start()
        started.append(copy)
        return copy

    def arrive(copies):
        for copy in copies:
            copy.wait_recv()

    order = (2, 1, 3)
    barrier = pltpu.get_barrier_semaphore()
    for d in (1, 2, 3):
        for device in (team(d), line(d)):
            pl.semaphore_signal(
                barrier, inc=1, device_id={"seq": device}, device_id_type=pl.DeviceIdType.MESH
            )
    pl.semaphore_wait(barrier, 6)

    c_win = [
        send(S_WIN, d, win_in.at[(g + d) % TEAM], win.at[rows(me, share)], team(d)) for d in order
    ]
    c_gain = [send(S_GAIN, d, gain_in, gains.at[me], team(d)) for d in order]
    win[rows(me, share)] = win_in[g]
    gains[me] = gain_in[...]
    arrive(c_win)
    win_own = rows(z, share * TEAM)
    c_win_z = [send(S_WIN_Z, d, win.at[win_own], win.at[win_own], line(d)) for d in order]
    c_frames = [send(S_FRAMES, d, frames_in, fr.at[rows(g, block)], team(d)) for d in order]
    arrive(c_gain)
    team_own = pl.ds(z * TEAM, TEAM)
    c_gain_z = [send(S_GAIN_Z, d, gains.at[team_own], gains.at[team_own], line(d)) for d in order]
    ids_own = pl.ds(pl.multiple_of(PAD + g * block, PAD), block)
    c_ids = [send(S_IDS, d, ids_in, idx.at[ids_own], team(d)) for d in order]
    c_prm = [send(S_PRM, d, prm_in, prm.at[z], line(d)) for d in order]
    prm[z] = prm_in[...]
    fr[rows(g, block)] = frames_in[...]
    idx[ids_own] = ids_in[...]
    og[rows(g, block)] = og_in[...]
    wout[rows(z, share)] = wout_in[...]
    arrive(c_ids)
    c_idh = [
        send(S_IDS_HALO, 1, idx.at[pl.ds(group, PAD)], idx.at[pl.ds(0, PAD)], line(1)),
        send(S_IDS_HALO, 3, idx.at[pl.ds(PAD, PAD)], idx.at[pl.ds(PAD + group, PAD)], line(3)),
    ]

    c_og = [send(S_OG, d, og_in, og.at[rows(g, block)], team(d)) for d in order]
    c_wout = [send(S_WOUT, d, wout_in, wout.at[rows(z, share)], line(d)) for d in order]
    arrive(c_gain_z)
    for j in range(width // 128):
        gvec[:, pl.ds(128 * j, 128)] = gains[2 * j] + gains[2 * j + 1]
    arrive(c_frames)

    @pl.loop(0, group // 32)
    def _(i):
        at = rows(i, 32)
        x = fr[at].astype(F32)
        centred = x - jnp.mean(x, axis=1, keepdims=True)
        r = lax.rsqrt(jnp.mean(centred * centred, axis=1, keepdims=True) + EPSILON)
        hat = centred * r
        lnhat[at] = hat
        rstd[at] = jnp.broadcast_to(r, (32, 128))
        lnx[at] = (hat * gvec[0:1, :]).astype(BF16)

    arrive(c_prm)
    prml[:, 0:128] = prm[0] + prm[1]
    prml[:, 128:256] = prm[2] + prm[3]
    arrive(c_idh)

    @pl.when(z == 0)
    def _():
        idx[pl.ds(0, PAD)] = jnp.full((PAD, 128), -1.0, F32)

    @pl.when(z == LINE - 1)
    def _():
        idx[pl.ds(PAD + group, PAD)] = jnp.full((PAD, 128), -1.0, F32)

    arrive(c_win_z)

    @pl.loop(0, TEAM)
    def _(i):
        at = rows(i, block)
        h = jnp.dot(lnx[at], win[...], preferred_element_type=F32)
        inner = pl.ds(pl.multiple_of(PAD + i * block, PAD), block)
        for t in range(2):
            lanes = slice(128 * t, 128 * t + 128)
            lh = h[:, 256 * t : 256 * t + 128]
            rg = jax.nn.sigmoid(h[:, 256 * t + 128 : 256 * t + 256])
            left[at, lanes] = lh
            gate[at, lanes] = rg
            gext[t, inner] = (lh * rg).astype(BF16).astype(F32)

    def halo(stage, ext):
        return [
            send(
                stage, 1, ext.at[:, pl.ds(group, PAD)], ext.at[:, pl.ds(0, PAD)], line(1)
            ),
            send(
                stage, 3, ext.at[:, pl.ds(PAD, PAD)], ext.at[:, pl.ds(PAD + group, PAD)], line(3)
            ),
        ]

    c_gh = halo(S_GLU_HALO, gext)
    chunks = group // ROWS

    def forward(c):
        at = rows(c, ROWS)
        own = idx[pl.ds(pl.multiple_of(PAD + c * ROWS, 8), ROWS)]
        total = [jnp.zeros((ROWS, 128), F32) for _ in range(2)]
        for k in range(31):
            there = pl.ds(c * ROWS + 1 + k, ROWS)
            same = idx[there] == own
            for t in range(2):
                term = jnp.where(same, gext[t, there], 0.0)
                total[t] = total[t] + prml[k : k + 1, 128 * t : 128 * t + 128] * term
        for t in range(2):
            conv[at, 128 * t : 128 * t + 128] = total[t]

    @pl.loop(1, chunks - 1)
    def _(c):
        forward(c)

    arrive(c_gh)

    @pl.loop(0, 2)
    def _(c):
        forward(c * (chunks - 1))

    part_mean = jnp.sum(conv[...], axis=0, keepdims=True) / group
    off = conv[...] - part_mean
    bst[0, 0] = jnp.broadcast_to(part_mean, (8, chan))
    bst[0, 1] = jnp.broadcast_to(jnp.sum(off * off, axis=0, keepdims=True), (8, chan))
    c_bn = [send(S_BN, d, bst.at[0], bst.at[d], line(d)) for d in order]

    arrive(c_wout)
    arrive(c_og)

    @pl.loop(0, TEAM)
    def _(i):
        at = rows(i, block)
        gact[at] = lax.dot_general(
            og[at], wout[...], (((1,), (1,)), ((), ())), preferred_element_type=F32
        )

    arrive(c_bn)
    means = [bst[d, 0] for d in range(LINE)]
    bn_mean8 = (means[0] + means[1] + means[2] + means[3]) / LINE
    spread = jnp.zeros((8, chan), F32)
    for d in range(LINE):
        shift = means[d] - bn_mean8
        spread = spread + bst[d, 1] + group * (shift * shift)
    bn_rstd = lax.rsqrt(spread / stream + EPSILON)[0:1]
    bn_mean = bn_mean8[0:1]
    bn_gain = prml[31:32, :]
    bn_bias = prml[32:33, :]

    def activate(i, sums):
        at = rows(i, ROWS)
        hat = (conv[at] - bn_mean) * bn_rstd
        zed = hat * bn_gain + bn_bias
        zg = jax.nn.sigmoid(zed)
        act[at] = (zed * zg).astype(BF16)
        gz = gact[at] * zg * (1.0 + zed * (1.0 - zg))
        conv[at] = hat
        gact[at] = gz
        fold = lambda v: jnp.sum(v.reshape(ROWS // 8, 8, chan), axis=0)
        return sums[0] + fold(gz), sums[1] + fold(gz * hat)

    zero = jnp.zeros((8, chan), F32)
    sums = lax.fori_loop(0, chunks, activate, (zero, zero))
    for j in range(2):
        bst2[0, j] = jnp.broadcast_to(jnp.sum(sums[j], axis=0, keepdims=True), (8, chan))
    c_bn2 = [send(S_BN_BACK, d, bst2.at[0], bst2.at[d], line(d)) for d in order]

    for j in range(2):
        edge = slice(j * (group - PAD), j * (group - PAD) + PAD)
        hs[j, 0] = gact[edge]
        hs[j, 1] = conv[edge]
    c_gc = [
        send(S_GC_HALO, 1, hs.at[1], hr.at[0], line(1)),
        send(S_GC_HALO, 3, hs.at[0], hr.at[1], line(3)),
    ]
    gwo = lax.dot_general(
        act[...], og[...], (((0,), (0,)), ((), ())), preferred_element_type=F32
    ).astype(BF16)
    for j in range(LINE):
        gwos[j] = gwo[j * share : (j + 1) * share]
    c_gwo = [send(S_GWOUT, d, gwos.at[(z + d) % LINE], gwor.at[d], line(d)) for d in order]

    @pl.loop(0, TEAM)
    def _(i):
        at = rows(i, block)
        projs[i] = jnp.dot(act[at], wout[...], preferred_element_type=F32).astype(BF16)

    c_proj = [send(S_PROJ, d, projs.at[(g + d) % TEAM], projr.at[d], team(d)) for d in order]

    arrive(c_bn2)
    bias_total = (bst2[0, 0] + bst2[1, 0] + bst2[2, 0] + bst2[3, 0])[0:1]
    gain_total = (bst2[0, 1] + bst2[1, 1] + bst2[2, 1] + bst2[3, 1])[0:1]
    gbn_ref[0] = jnp.broadcast_to(gain_total * scale, (8, chan))
    gbn_ref[1] = jnp.broadcast_to(bias_total * scale, (8, chan))
    lead = bn_gain * bn_rstd
    bias_mean = bias_total / stream
    gain_mean = gain_total / stream

    def store_gc(inner, grad, hat):
        gc = lead * (grad - bias_mean - hat * gain_mean)
        gcext[0, inner] = gc[:, :128]
        gcext[1, inner] = gc[:, 128:]

    @pl.loop(0, chunks)
    def _(i):
        at = rows(i, ROWS)
        store_gc(pl.ds(pl.multiple_of(PAD + i * ROWS, PAD), ROWS), gact[at], conv[at])

    arrive(c_gc)
    store_gc(pl.ds(0, PAD), hr[0, 0], hr[0, 1])
    store_gc(pl.ds(PAD + group, PAD), hr[1, 0], hr[1, 1])

    gkacc[...] = jnp.zeros_like(gkacc)

    def backward(c, t):
        at = rows(c, ROWS)
        inner = pl.ds(pl.multiple_of(PAD + c * ROWS, 8), ROWS)
        lanes = slice(128 * t, 128 * t + 128)
        own = idx[inner]
        value = gext[t, inner]
        total = jnp.zeros((ROWS, 128), F32)
        for j in range(31):
            k = 30 - j
            there = pl.ds(c * ROWS + 1 + j, ROWS)
            term = jnp.where(idx[there] == own, gcext[t, there], 0.0)
            total = total + prml[k : k + 1, lanes] * term
            fold = jnp.sum((value * term).reshape(ROWS // 8, 8, 128), axis=0)
            gkacc[k, :, lanes] = gkacc[k, :, lanes] + fold
        rg = gate[at, lanes]
        gh[at, 256 * t : 256 * t + 128] = (total * rg).astype(BF16)
        gh[at, 256 * t + 128 : 256 * t + 256] = (total * left[at, lanes] * rg * (1.0 - rg)).astype(
            BF16
        )

    c_gwi = []
    for t in range(2):

        @pl.loop(0, chunks)
        def _(c):
            backward(c, t)

        copies = []
        for d in (2, 1, 3, 0):
            gwis[t, d] = lax.dot_general(
                lnx[:, rows((z + d) % LINE, chan)],
                gh[:, 256 * t : 256 * t + 256],
                (((0,), (0,)), ((), ())),
                preferred_element_type=F32,
            ).astype(BF16)
            if d:
                copies.append(
                    send((S_GWIN, S_GWIN_B)[t], d, gwis.at[t, d], gwir.at[t, d], line(d))
                )
        c_gwi.append(copies)

    for t in range(2):
        gkr[t] = jnp.sum(gkacc[:, :, 128 * t : 128 * t + 128], axis=1)
    c_gk = [send(S_GK, d, gkr.at[((z + d) % LINE) // 2], gkrecv.at[d], line(d)) for d in order]

    def lower(i, total):
        at = rows(i, block)
        part = lax.dot_general(
            gh[at], win[...], (((1,), (1,)), ((), ())), preferred_element_type=F32
        )
        glns[i] = part.astype(BF16)
        return total + jnp.sum(part * lnhat[at], axis=0, keepdims=True)

    gg = lax.fori_loop(0, TEAM, lower, jnp.zeros((1, width), F32))
    c_gln = [send(S_GLN, d, glns.at[(g + d) % TEAM], glnr.at[d], team(d)) for d in order]
    for j in range(LINE):
        ggs[j] = jnp.broadcast_to(gg[:, j * chan : (j + 1) * chan], (8, chan))
    c_gg = [send(S_GGAIN, d, ggs.at[(z + d) % LINE], ggr.at[d], line(d)) for d in order]

    arrive(c_proj)
    o = frames_in[...].astype(F32) + projs[g].astype(F32)
    for d in (1, 2, 3):
        o = o + projr[d].astype(F32)
    out_ref[...] = o.astype(BF16)
    arrive(c_gwo)
    o = gwos[z].astype(F32)
    for d in (1, 2, 3):
        o = o + gwor[d].astype(F32)
    gwout_ref[...] = o * scale
    arrive(c_gk)
    gk_ref[...] = (gkr[z // 2] + gkrecv[1] + gkrecv[2] + gkrecv[3]) * scale

    arrive(c_gg)
    gs = ggs[z] + ggr[1] + ggr[2] + ggr[3]
    ggt[0] = gs[:, :128]
    ggt[1] = gs[:, 128:]
    c_ggt = [send(S_GGAIN_T, d, ggt.at[((g + d) % TEAM) // 2], ggtr.at[d], team(d)) for d in order]

    arrive(c_gln)

    @pl.loop(0, block // 32)
    def _(i):
        at = rows(i, 32)
        there = pl.ds(pl.multiple_of(g * block + i * 32, 32), 32)
        gl = glns[g, at].astype(F32)
        for d in (1, 2, 3):
            gl = gl + glnr[d, at].astype(F32)
        hat = lnhat[there]
        ghat = gl * gvec[0:1, :]
        gx = rstd[there][:, 0:1] * (
            ghat
            - jnp.mean(ghat, axis=1, keepdims=True)
            - hat * jnp.mean(ghat * hat, axis=1, keepdims=True)
        )
        gframes_ref[at] = (og_in[at].astype(F32) + gx).astype(BF16)

    c_gwt = []
    for t in range(2):
        arrive(c_gwi[t])
        o = gwis[t, 0].astype(F32)
        for d in (1, 2, 3):
            o = o + gwir[t, d].astype(F32)
        o = o.astype(BF16)
        for j in range(TEAM):
            gwit[t, j] = o[j * share : (j + 1) * share]
        c_gwt += [
            send(
                (S_GWIN_T, S_GWIN_TB)[t],
                d,
                gwit.at[t, (g + d) % TEAM],
                gwitr.at[t, g],
                team(d),
            )
            for d in order
        ]
        gwitr[t, g] = gwit[t, g]
    arrive(c_ggt)
    ggain_ref[...] = (ggt[g // 2] + ggtr[1] + ggtr[2] + ggtr[3]) * scale
    arrive(c_gwt)
    low = lax.broadcasted_iota(jnp.int32, (share, 128), 1) < share
    for t in range(2):
        for half in range(2):
            lanes = slice(128 * half, 128 * half + 128)
            for p in range(2):
                even = gwitr[t, 2 * p][:, lanes].astype(F32) * scale
                odd = gwitr[t, 2 * p + 1][:, lanes].astype(F32) * scale
                at = half * width + 2 * t * chan + 128 * p
                gwin_ref[:, at : at + 128] = jnp.where(low, even, pltpu.roll(odd, share, 1))
                gwin_ref[:, at + chan : at + chan + 128] = jnp.where(
                    low, pltpu.roll(even, share, 1), odd
                )
    for copy in started:
        copy.wait_send()


def fused(frames, segment_ids, out_grad, ln_gain, w_in, dw_kernel, bn_gain, bn_bias, w_out):
    block, width = frames.shape
    share = w_in.shape[0]
    group = block * TEAM
    chan = width // TEAM
    me = lax.axis_index("seq")
    z, g = me // TEAM, me % TEAM
    ids = jnp.broadcast_to(segment_ids.astype(F32)[:, None], (block, 128))
    lane_half = jnp.arange(128) // share

    def halves(rows_, odd):
        both = jnp.concatenate([rows_, rows_], axis=1)
        return jnp.where(lane_half[None, :] == odd, both, 0.0)

    gain = halves(jnp.broadcast_to(ln_gain[None, :], (8, share)), g % 2)
    prm = halves(
        jnp.concatenate(
            [dw_kernel, bn_gain[None], bn_bias[None], jnp.zeros((7, share), F32)], axis=0
        ),
        z % 2,
    )
    win = (
        w_in.reshape(share, 2, 2, 2, TEAM, share)
        .transpose(4, 0, 2, 1, 3, 5)
        .reshape(TEAM, share, 2 * chan)
    )
    vmem = pl.BlockSpec(memory_space=pltpu.VMEM)
    shape = jax.ShapeDtypeStruct
    ext = group + 2 * PAD
    out, gframes, gwin, gwout, gk, ggain, gbn = pl.pallas_call(
        fused_kernel,
        out_shape=[
            shape((block, width), BF16),
            shape((block, width), BF16),
            shape((share, 2 * width), F32),
            shape((share, width), F32),
            shape((32, 128), F32),
            shape((8, 128), F32),
            shape((2, 8, chan), F32),
        ],
        in_specs=[vmem] * 7,
        out_specs=[vmem] * 7,
        scratch_shapes=[
            pltpu.VMEM((group, width), BF16),
            pltpu.VMEM((ext, 128), F32),
            pltpu.VMEM((group, width), BF16),
            pltpu.VMEM((TEAM * LINE, 8, 128), F32),
            pltpu.VMEM((8, width), F32),
            pltpu.VMEM((width, 2 * chan), BF16),
            pltpu.VMEM((LINE, 40, 128), F32),
            pltpu.VMEM((40, chan), F32),
            pltpu.VMEM((chan, width), BF16),
            pltpu.VMEM((group, width), F32),
            pltpu.VMEM((group, 128), F32),
            pltpu.VMEM((group, width), BF16),
            pltpu.VMEM((group, chan), F32),
            pltpu.VMEM((group, chan), F32),
            pltpu.VMEM((2, ext, 128), F32),
            pltpu.VMEM((group, chan), F32),
            pltpu.VMEM((group, chan), F32),
            pltpu.VMEM((group, chan), BF16),
            pltpu.VMEM((LINE, 2, 8, chan), F32),
            pltpu.VMEM((LINE, 2, 8, chan), F32),
            pltpu.VMEM((2, ext, 128), F32),
            pltpu.VMEM((group, 2 * chan), BF16),
            pltpu.VMEM((2, 2, PAD, chan), F32),
            pltpu.VMEM((2, 2, PAD, chan), F32),
            pltpu.VMEM((32, 8, chan), F32),
            pltpu.VMEM((2, 32, 128), F32),
            pltpu.VMEM((LINE, 32, 128), F32),
            pltpu.VMEM((TEAM, block, width), BF16),
            pltpu.VMEM((TEAM, block, width), BF16),
            pltpu.VMEM((LINE, share, width), BF16),
            pltpu.VMEM((LINE, share, width), BF16),
            pltpu.VMEM((2, LINE, chan, chan), BF16),
            pltpu.VMEM((2, LINE, chan, chan), BF16),
            pltpu.VMEM((2, TEAM, share, chan), BF16),
            pltpu.VMEM((2, TEAM, share, chan), BF16),
            pltpu.VMEM((TEAM, block, width), BF16),
            pltpu.VMEM((TEAM, block, width), BF16),
            pltpu.VMEM((LINE, 8, chan), F32),
            pltpu.VMEM((LINE, 8, chan), F32),
            pltpu.VMEM((2, 8, 128), F32),
            pltpu.VMEM((TEAM, 8, 128), F32),
            pltpu.SemaphoreType.DMA((STAGES, 4)),
            pltpu.SemaphoreType.DMA((STAGES, 4)),
        ],
        compiler_params=pltpu.CompilerParams(
            collective_id=0, has_side_effects=True, vmem_limit_bytes=48 * 1024 * 1024
        ),
    )(frames, ids, out_grad, gain, win, prm, w_out)
    gk = jnp.where(z % 2 == 0, gk[:31, :share], gk[:31, share:])
    ggain = jnp.where(g % 2 == 0, ggain[0, :share], ggain[0, share:])
    gbn = lax.dynamic_slice_in_dim(gbn[:, 0, :], z * share, share, 1)
    return out, gframes, gwin, gwout, gk, ggain, gbn[0], gbn[1]


def solution(mesh):
    small = mesh.shape["seq"] == TEAM * LINE
    return jax.shard_map(
        fused if small else local,
        mesh=mesh,
        in_specs=(
            P(("mix", "seq"), None),
            P(("mix", "seq")),
            P(("mix", "seq"), None),
            P(("mix", "seq")),
            P(("mix", "seq"), None),
            P("mix", "seq"),
            P(("mix", "seq")),
            P(("mix", "seq")),
            P(("mix", "seq"), None),
        ),
        out_specs=(
            P(("mix", "seq"), None),
            P(("mix", "seq"), None),
            P(("mix", "seq"), None),
            P(("mix", "seq"), None),
            P("mix", "seq"),
            P(("mix", "seq")),
            P(("mix", "seq")),
            P(("mix", "seq")),
        ),
        check_vma=False,
    )
```

```python
import math

import jax
import jax.numpy as jnp
from jax import lax
from jax.experimental import pallas as pl
from jax.experimental.pallas import tpu as pltpu
from jax.sharding import PartitionSpec as P

EPSILON = 1e-05


def with_halo(cells, sides, width):
    for axis, dim in sides:
        count = lax.axis_size(axis)
        ends = count - 1
        head = lax.slice_in_dim(cells, 0, width, axis=dim)
        tail = lax.slice_in_dim(cells, cells.shape[dim] - width, cells.shape[dim], axis=dim)
        cells = jnp.concatenate(
            [
                lax.ppermute(tail, axis, [(i, (i + 1) % count) for i in range(ends)]),
                cells,
                lax.ppermute(head, axis, [((i + 1) % count, i) for i in range(ends)]),
            ],
            axis=dim,
        )
    return cells


def local(frames, segment_ids, out_grad, ln_gain, w_in, dw_kernel, bn_gain, bn_bias, w_out):
    frame_count = frames.shape[0]
    width = frames.shape[1]
    taps = dw_kernel.shape[0]
    margin = taps // 2
    devices = lax.axis_size("seq")
    stream = frame_count * devices
    grad_scale = 1.0 / math.sqrt(stream)
    share = width // devices
    gains, kernel, bn_scale, bn_shift = (
        lax.all_gather(ln_gain, "seq", axis=0, tiled=True),
        lax.all_gather(dw_kernel, "seq", axis=1, tiled=True),
        lax.all_gather(bn_gain, "seq", axis=0, tiled=True),
        lax.all_gather(bn_bias, "seq", axis=0, tiled=True),
    )
    own_ids = segment_ids + 1
    padded_ids = with_halo(own_ids, (("seq", 0),), margin)
    masks = [
        (padded_ids[tap_index : tap_index + frame_count] == own_ids).astype(jnp.float32)[:, None]
        for tap_index in range(taps)
    ]
    frames_float = frames.astype(jnp.float32)
    mean_ln = jnp.mean(frames_float, axis=1, keepdims=True)
    centred = frames_float - mean_ln
    rstd_ln = lax.rsqrt(jnp.mean(centred * centred, axis=1, keepdims=True) + EPSILON)
    ln_hat = centred * rstd_ln
    ln_x = (ln_hat * gains).astype(jnp.bfloat16)
    columns = ln_x
    hidden = jnp.dot(
        columns, lax.all_gather(w_in, "seq", axis=0, tiled=True), preferred_element_type=jnp.float32
    )
    left_half = hidden[:, :width]
    right_gate = jax.nn.sigmoid(hidden[:, width:])
    glu = (left_half * right_gate).astype(jnp.bfloat16)
    padded_glu = with_halo(glu, (("seq", 0),), margin)
    conv_out = jnp.zeros((frame_count, width), jnp.float32)
    for tap_index in range(taps):
        conv_out = (
            conv_out
            + kernel[tap_index]
            * padded_glu[tap_index : tap_index + frame_count].astype(jnp.float32)
            * masks[tap_index]
        )
    plain_sums, square_sums = lax.psum(
        (jnp.sum(conv_out, axis=0), jnp.sum(conv_out * conv_out, axis=0)), "seq"
    )
    bn_mean = plain_sums / stream
    bn_var = square_sums / stream - bn_mean * bn_mean
    bn_rstd = lax.rsqrt(bn_var + EPSILON)
    bn_hat = (conv_out - bn_mean) * bn_rstd
    zed = bn_hat * bn_scale + bn_shift
    zed_gate = jax.nn.sigmoid(zed)
    activation = (zed * zed_gate).astype(jnp.bfloat16)
    columns = activation
    projected = jnp.dot(
        columns,
        lax.all_gather(w_out, "seq", axis=0, tiled=True),
        preferred_element_type=jnp.float32,
    )
    outputs = (frames_float + projected).astype(jnp.bfloat16)
    grad_w_out = lax.psum_scatter(
        jnp.einsum("fa,fb->ab", activation, out_grad, preferred_element_type=jnp.float32)
        * grad_scale,
        "seq",
        scatter_dimension=0,
        tiled=True,
    )
    grad_act = jnp.einsum(
        "fe,ne->fn",
        out_grad,
        lax.all_gather(w_out, "seq", axis=0, tiled=True),
        preferred_element_type=jnp.float32,
    )
    grad_zed = grad_act * zed_gate * (1.0 + zed * (1.0 - zed_gate))
    bias_total, gain_total = lax.psum(
        (jnp.sum(grad_zed, axis=0), jnp.sum(grad_zed * bn_hat, axis=0)), "seq"
    )
    grad_conv = bn_scale * bn_rstd * (grad_zed - bias_total / stream - bn_hat * gain_total / stream)
    first_channel = lax.axis_index("seq") * share
    grad_bn_bias = lax.dynamic_slice_in_dim(bias_total, first_channel, share, 0) * grad_scale
    grad_bn_gain = lax.dynamic_slice_in_dim(gain_total, first_channel, share, 0) * grad_scale
    kernel_rows = [
        jnp.sum(
            grad_conv
            * padded_glu[tap_index : tap_index + frame_count].astype(jnp.float32)
            * masks[tap_index],
            axis=0,
        )
        for tap_index in range(taps)
    ]
    kernel_term = jnp.stack(kernel_rows) * grad_scale
    padded_conv = with_halo(grad_conv, (("seq", 0),), margin)
    grad_glu = jnp.zeros((frame_count, width), jnp.float32)
    for tap_index in range(taps):
        mirror = 2 * margin - tap_index
        grad_glu = (
            grad_glu
            + kernel[tap_index] * padded_conv[mirror : mirror + frame_count] * masks[mirror]
        )
    grad_hidden = jnp.concatenate(
        [grad_glu * right_gate, grad_glu * left_half * right_gate * (1.0 - right_gate)], axis=1
    ).astype(jnp.bfloat16)
    grad_ln = jnp.einsum(
        "fe,ne->fn",
        grad_hidden,
        lax.all_gather(w_in, "seq", axis=0, tiled=True),
        preferred_element_type=jnp.float32,
    )
    in_term = (
        jnp.einsum("fa,fb->ab", ln_x, grad_hidden, preferred_element_type=jnp.float32) * grad_scale
    )
    gain_term = jnp.sum(grad_ln * ln_hat, axis=0) * grad_scale
    grad_w_in, grad_kernel, grad_ln_gain = (
        lax.psum_scatter(in_term, "seq", scatter_dimension=0, tiled=True),
        lax.psum_scatter(kernel_term, "seq", scatter_dimension=1, tiled=True),
        lax.psum_scatter(gain_term, "seq", scatter_dimension=0, tiled=True),
    )
    grad_hat = grad_ln * gains
    grad_input = rstd_ln * (
        grad_hat
        - jnp.mean(grad_hat, axis=1, keepdims=True)
        - ln_hat * jnp.mean(grad_hat * ln_hat, axis=1, keepdims=True)
    )
    grad_frames = (out_grad.astype(jnp.float32) + grad_input).astype(jnp.bfloat16)
    return (
        outputs,
        grad_frames,
        grad_w_in,
        grad_w_out,
        grad_kernel,
        grad_ln_gain,
        grad_bn_gain,
        grad_bn_bias,
    )


TEAM = 4
LINE = 4
PAD = 16
ROWS = 64
(
    S_WIN,
    S_GAIN,
    S_FRAMES,
    S_IDS,
    S_OG,
    S_WIN_Z,
    S_GAIN_Z,
    S_PRM,
    S_WOUT,
    S_IDS_HALO,
    S_GLU_HALO,
    S_BN,
    S_BN_BACK,
    S_GC_HALO,
    S_PROJ,
    S_GWOUT,
    S_GK,
    S_GWIN,
    S_GGAIN,
    S_GLN,
    S_GWIN_T,
    S_GGAIN_T,
    S_GWIN_B,
    S_GWIN_TB,
    STAGES,
) = range(25)
F32 = jnp.float32
BF16 = jnp.bfloat16


def fused_kernel(
    frames_in,
    ids_in,
    og_in,
    gain_in,
    win_in,
    prm_in,
    wout_in,
    out_ref,
    gframes_ref,
    gwin_ref,
    gwout_ref,
    gk_ref,
    ggain_ref,
    gbn_ref,
    fr,
    idx,
    og,
    gains,
    gvec,
    win,
    prm,
    prml,
    wout,
    lnhat,
    rstd,
    lnx,
    left,
    gate,
    gext,
    conv,
    gact,
    act,
    bst,
    bst2,
    gcext,
    gh,
    hs,
    hr,
    gkacc,
    gkr,
    gkrecv,
    projs,
    projr,
    gwos,
    gwor,
    gwis,
    gwir,
    gwit,
    gwitr,
    glns,
    glnr,
    ggs,
    ggr,
    ggt,
    ggtr,
    send_sem,
    recv_sem,
):
    block, width = frames_in.shape
    group = block * TEAM
    chan = width // TEAM
    share = wout_in.shape[0]
    stream = group * LINE
    scale = 1.0 / math.sqrt(stream)
    me = lax.axis_index("seq")
    z, g = me // TEAM, me % TEAM

    def team(d):
        return z * TEAM + (g + d) % TEAM

    def line(d):
        return ((z + d) % LINE) * TEAM + g

    def rows(i, n):
        return pl.ds(pl.multiple_of(i * n, n), n)

    started = []

    def send(stage, d, source, target, device):
        copy = pltpu.make_async_remote_copy(
            src_ref=source,
            dst_ref=target,
            send_sem=send_sem.at[stage, d],
            recv_sem=recv_sem.at[stage, d],
            device_id={"seq": device},
            device_id_type=pl.DeviceIdType.MESH,
        )
        copy.start()
        started.append(copy)
        return copy

    def arrive(copies):
        for copy in copies:
            copy.wait_recv()

    order = (2, 1, 3)
    barrier = pltpu.get_barrier_semaphore()
    for d in (1, 2, 3):
        for device in (team(d), line(d)):
            pl.semaphore_signal(
                barrier, inc=1, device_id={"seq": device}, device_id_type=pl.DeviceIdType.MESH
            )
    pl.semaphore_wait(barrier, 6)

    c_win = [
        send(S_WIN, d, win_in.at[(g + d) % TEAM], win.at[rows(me, share)], team(d)) for d in order
    ]
    c_gain = [send(S_GAIN, d, gain_in, gains.at[me], team(d)) for d in order]
    win[rows(me, share)] = win_in[g]
    gains[me] = gain_in[...]
    arrive(c_win)
    win_own = rows(z, share * TEAM)
    c_win_z = [send(S_WIN_Z, d, win.at[win_own], win.at[win_own], line(d)) for d in order]
    c_frames = [send(S_FRAMES, d, frames_in, fr.at[rows(g, block)], team(d)) for d in order]
    arrive(c_gain)
    team_own = pl.ds(z * TEAM, TEAM)
    c_gain_z = [send(S_GAIN_Z, d, gains.at[team_own], gains.at[team_own], line(d)) for d in order]
    ids_own = pl.ds(pl.multiple_of(PAD + g * block, PAD), block)
    c_ids = [send(S_IDS, d, ids_in, idx.at[ids_own], team(d)) for d in order]
    c_prm = [send(S_PRM, d, prm_in, prm.at[z], line(d)) for d in order]
    prm[z] = prm_in[...]
    fr[rows(g, block)] = frames_in[...]
    idx[ids_own] = ids_in[...]
    og[rows(g, block)] = og_in[...]
    wout[rows(z, share)] = wout_in[...]
    arrive(c_ids)
    c_idh = [
        send(S_IDS_HALO, 1, idx.at[pl.ds(group, PAD)], idx.at[pl.ds(0, PAD)], line(1)),
        send(S_IDS_HALO, 3, idx.at[pl.ds(PAD, PAD)], idx.at[pl.ds(PAD + group, PAD)], line(3)),
    ]

    arrive(c_gain_z)
    for j in range(width // 128):
        gvec[:, pl.ds(128 * j, 128)] = gains[2 * j] + gains[2 * j + 1]
    arrive(c_frames)
    c_og = [send(S_OG, d, og_in, og.at[rows(g, block)], team(d)) for d in order]

    @pl.loop(0, group // 32)
    def _(i):
        at = rows(i, 32)
        x = fr[at].astype(F32)
        centred = x - jnp.mean(x, axis=1, keepdims=True)
        r = lax.rsqrt(jnp.mean(centred * centred, axis=1, keepdims=True) + EPSILON)
        hat = centred * r
        lnhat[at] = hat
        rstd[at] = jnp.broadcast_to(r, (32, 128))
        lnx[at] = (hat * gvec[0:1, :]).astype(BF16)

    arrive(c_prm)
    prml[:, 0:128] = prm[0] + prm[1]
    prml[:, 128:256] = prm[2] + prm[3]
    arrive(c_idh)

    @pl.when(z == 0)
    def _():
        idx[pl.ds(0, PAD)] = jnp.full((PAD, 128), -1.0, F32)

    @pl.when(z == LINE - 1)
    def _():
        idx[pl.ds(PAD + group, PAD)] = jnp.full((PAD, 128), -1.0, F32)

    arrive(c_win_z)
    c_wout = [send(S_WOUT, d, wout_in, wout.at[rows(z, share)], line(d)) for d in order]

    @pl.loop(0, TEAM)
    def _(i):
        at = rows(i, block)
        h = jnp.dot(lnx[at], win[...], preferred_element_type=F32)
        inner = pl.ds(pl.multiple_of(PAD + i * block, PAD), block)
        for t in range(2):
            lanes = slice(128 * t, 128 * t + 128)
            lh = h[:, 256 * t : 256 * t + 128]
            rg = jax.nn.sigmoid(h[:, 256 * t + 128 : 256 * t + 256])
            left[at, lanes] = lh
            gate[at, lanes] = rg
            gext[t, inner] = (lh * rg).astype(BF16).astype(F32)

    def halo(stage, ext):
        return [
            send(
                stage, 1, ext.at[:, pl.ds(group, PAD)], ext.at[:, pl.ds(0, PAD)], line(1)
            ),
            send(
                stage, 3, ext.at[:, pl.ds(PAD, PAD)], ext.at[:, pl.ds(PAD + group, PAD)], line(3)
            ),
        ]

    c_gh = halo(S_GLU_HALO, gext)
    chunks = group // ROWS

    def forward(c):
        at = rows(c, ROWS)
        own = idx[pl.ds(pl.multiple_of(PAD + c * ROWS, 8), ROWS)]
        total = [jnp.zeros((ROWS, 128), F32) for _ in range(2)]
        for k in range(31):
            there = pl.ds(c * ROWS + 1 + k, ROWS)
            same = idx[there] == own
            for t in range(2):
                term = jnp.where(same, gext[t, there], 0.0)
                total[t] = total[t] + prml[k : k + 1, 128 * t : 128 * t + 128] * term
        for t in range(2):
            conv[at, 128 * t : 128 * t + 128] = total[t]

    @pl.loop(1, chunks - 1)
    def _(c):
        forward(c)

    arrive(c_gh)

    @pl.loop(0, 2)
    def _(c):
        forward(c * (chunks - 1))

    part_mean = jnp.sum(conv[...], axis=0, keepdims=True) / group
    off = conv[...] - part_mean
    bst[0, 0] = jnp.broadcast_to(part_mean, (8, chan))
    bst[0, 1] = jnp.broadcast_to(jnp.sum(off * off, axis=0, keepdims=True), (8, chan))
    c_bn = [send(S_BN, d, bst.at[0], bst.at[d], line(d)) for d in order]

    arrive(c_wout)
    arrive(c_og)

    @pl.loop(0, TEAM)
    def _(i):
        at = rows(i, block)
        gact[at] = lax.dot_general(
            og[at], wout[...], (((1,), (1,)), ((), ())), preferred_element_type=F32
        )

    arrive(c_bn)
    means = [bst[d, 0] for d in range(LINE)]
    bn_mean8 = (means[0] + means[1] + means[2] + means[3]) / LINE
    spread = jnp.zeros((8, chan), F32)
    for d in range(LINE):
        shift = means[d] - bn_mean8
        spread = spread + bst[d, 1] + group * (shift * shift)
    bn_rstd = lax.rsqrt(spread / stream + EPSILON)[0:1]
    bn_mean = bn_mean8[0:1]
    bn_gain = prml[31:32, :]
    bn_bias = prml[32:33, :]

    def activate(i, sums):
        at = rows(i, ROWS)
        hat = (conv[at] - bn_mean) * bn_rstd
        zed = hat * bn_gain + bn_bias
        zg = jax.nn.sigmoid(zed)
        act[at] = (zed * zg).astype(BF16)
        gz = gact[at] * zg * (1.0 + zed * (1.0 - zg))
        conv[at] = hat
        gact[at] = gz
        fold = lambda v: jnp.sum(v.reshape(ROWS // 8, 8, chan), axis=0)
        return sums[0] + fold(gz), sums[1] + fold(gz * hat)

    zero = jnp.zeros((8, chan), F32)
    sums = lax.fori_loop(0, chunks, activate, (zero, zero))
    for j in range(2):
        bst2[0, j] = jnp.broadcast_to(jnp.sum(sums[j], axis=0, keepdims=True), (8, chan))
    c_bn2 = [send(S_BN_BACK, d, bst2.at[0], bst2.at[d], line(d)) for d in order]

    for j in range(2):
        edge = slice(j * (group - PAD), j * (group - PAD) + PAD)
        hs[j, 0] = gact[edge]
        hs[j, 1] = conv[edge]
    c_gc = [
        send(S_GC_HALO, 1, hs.at[1], hr.at[0], line(1)),
        send(S_GC_HALO, 3, hs.at[0], hr.at[1], line(3)),
    ]
    gwo = lax.dot_general(
        act[...], og[...], (((0,), (0,)), ((), ())), preferred_element_type=F32
    ).astype(BF16)
    for j in range(LINE):
        gwos[j] = gwo[j * share : (j + 1) * share]
    c_gwo = [send(S_GWOUT, d, gwos.at[(z + d) % LINE], gwor.at[d], line(d)) for d in order]

    @pl.loop(0, TEAM)
    def _(i):
        at = rows(i, block)
        projs[i] = jnp.dot(act[at], wout[...], preferred_element_type=F32).astype(BF16)

    c_proj = [send(S_PROJ, d, projs.at[(g + d) % TEAM], projr.at[d], team(d)) for d in order]

    arrive(c_bn2)
    bias_total = (bst2[0, 0] + bst2[1, 0] + bst2[2, 0] + bst2[3, 0])[0:1]
    gain_total = (bst2[0, 1] + bst2[1, 1] + bst2[2, 1] + bst2[3, 1])[0:1]
    gbn_ref[0] = jnp.broadcast_to(gain_total * scale, (8, chan))
    gbn_ref[1] = jnp.broadcast_to(bias_total * scale, (8, chan))
    lead = bn_gain * bn_rstd
    bias_mean = bias_total / stream
    gain_mean = gain_total / stream

    def store_gc(inner, grad, hat):
        gc = lead * (grad - bias_mean - hat * gain_mean)
        gcext[0, inner] = gc[:, :128]
        gcext[1, inner] = gc[:, 128:]

    @pl.loop(0, chunks)
    def _(i):
        at = rows(i, ROWS)
        store_gc(pl.ds(pl.multiple_of(PAD + i * ROWS, PAD), ROWS), gact[at], conv[at])

    arrive(c_gc)
    store_gc(pl.ds(0, PAD), hr[0, 0], hr[0, 1])
    store_gc(pl.ds(PAD + group, PAD), hr[1, 0], hr[1, 1])

    gkacc[...] = jnp.zeros_like(gkacc)

    def backward(c, t):
        at = rows(c, ROWS)
        inner = pl.ds(pl.multiple_of(PAD + c * ROWS, 8), ROWS)
        lanes = slice(128 * t, 128 * t + 128)
        own = idx[inner]
        value = gext[t, inner]
        total = jnp.zeros((ROWS, 128), F32)
        for j in range(31):
            k = 30 - j
            there = pl.ds(c * ROWS + 1 + j, ROWS)
            term = jnp.where(idx[there] == own, gcext[t, there], 0.0)
            total = total + prml[k : k + 1, lanes] * term
            fold = jnp.sum((value * term).reshape(ROWS // 8, 8, 128), axis=0)
            gkacc[k, :, lanes] = gkacc[k, :, lanes] + fold
        rg = gate[at, lanes]
        gh[at, 256 * t : 256 * t + 128] = (total * rg).astype(BF16)
        gh[at, 256 * t + 128 : 256 * t + 256] = (total * left[at, lanes] * rg * (1.0 - rg)).astype(
            BF16
        )

    c_gwi = []
    for t in range(2):

        @pl.loop(0, chunks)
        def _(c):
            backward(c, t)

        copies = []
        for d in (2, 1, 3, 0):
            gwis[t, d] = lax.dot_general(
                lnx[:, rows((z + d) % LINE, chan)],
                gh[:, 256 * t : 256 * t + 256],
                (((0,), (0,)), ((), ())),
                preferred_element_type=F32,
            ).astype(BF16)
            if d:
                copies.append(
                    send((S_GWIN, S_GWIN_B)[t], d, gwis.at[t, d], gwir.at[t, d], line(d))
                )
        c_gwi.append(copies)

    for t in range(2):
        gkr[t] = jnp.sum(gkacc[:, :, 128 * t : 128 * t + 128], axis=1)
    c_gk = [send(S_GK, d, gkr.at[((z + d) % LINE) // 2], gkrecv.at[d], line(d)) for d in order]

    def lower(i, total):
        at = rows(i, block)
        part = lax.dot_general(
            gh[at], win[...], (((1,), (1,)), ((), ())), preferred_element_type=F32
        )
        glns[i] = part.astype(BF16)
        return total + jnp.sum(part * lnhat[at], axis=0, keepdims=True)

    gg = lax.fori_loop(0, TEAM, lower, jnp.zeros((1, width), F32))
    c_gln = [send(S_GLN, d, glns.at[(g + d) % TEAM], glnr.at[d], team(d)) for d in order]
    for j in range(LINE):
        ggs[j] = jnp.broadcast_to(gg[:, j * chan : (j + 1) * chan], (8, chan))
    c_gg = [send(S_GGAIN, d, ggs.at[(z + d) % LINE], ggr.at[d], line(d)) for d in order]

    arrive(c_proj)
    o = frames_in[...].astype(F32) + projs[g].astype(F32)
    for d in (1, 2, 3):
        o = o + projr[d].astype(F32)
    out_ref[...] = o.astype(BF16)
    arrive(c_gwo)
    o = gwos[z].astype(F32)
    for d in (1, 2, 3):
        o = o + gwor[d].astype(F32)
    gwout_ref[...] = o * scale
    arrive(c_gk)
    gk_ref[...] = (gkr[z // 2] + gkrecv[1] + gkrecv[2] + gkrecv[3]) * scale

    arrive(c_gg)
    gs = ggs[z] + ggr[1] + ggr[2] + ggr[3]
    ggt[0] = gs[:, :128]
    ggt[1] = gs[:, 128:]
    c_ggt = [send(S_GGAIN_T, d, ggt.at[((g + d) % TEAM) // 2], ggtr.at[d], team(d)) for d in order]

    arrive(c_gln)

    @pl.loop(0, block // 32)
    def _(i):
        at = rows(i, 32)
        there = pl.ds(pl.multiple_of(g * block + i * 32, 32), 32)
        gl = glns[g, at].astype(F32)
        for d in (1, 2, 3):
            gl = gl + glnr[d, at].astype(F32)
        hat = lnhat[there]
        ghat = gl * gvec[0:1, :]
        gx = rstd[there][:, 0:1] * (
            ghat
            - jnp.mean(ghat, axis=1, keepdims=True)
            - hat * jnp.mean(ghat * hat, axis=1, keepdims=True)
        )
        gframes_ref[at] = (og_in[at].astype(F32) + gx).astype(BF16)

    c_gwt = []
    for t in range(2):
        arrive(c_gwi[t])
        o = gwis[t, 0].astype(F32)
        for d in (1, 2, 3):
            o = o + gwir[t, d].astype(F32)
        o = o.astype(BF16)
        for j in range(TEAM):
            gwit[t, j] = o[j * share : (j + 1) * share]
        c_gwt += [
            send(
                (S_GWIN_T, S_GWIN_TB)[t],
                d,
                gwit.at[t, (g + d) % TEAM],
                gwitr.at[t, g],
                team(d),
            )
            for d in order
        ]
        gwitr[t, g] = gwit[t, g]
    arrive(c_ggt)
    ggain_ref[...] = (ggt[g // 2] + ggtr[1] + ggtr[2] + ggtr[3]) * scale
    arrive(c_gwt)
    low = lax.broadcasted_iota(jnp.int32, (share, 128), 1) < share
    for t in range(2):
        for half in range(2):
            lanes = slice(128 * half, 128 * half + 128)
            for p in range(2):
                even = gwitr[t, 2 * p][:, lanes].astype(F32) * scale
                odd = gwitr[t, 2 * p + 1][:, lanes].astype(F32) * scale
                at = half * width + 2 * t * chan + 128 * p
                gwin_ref[:, at : at + 128] = jnp.where(low, even, pltpu.roll(odd, share, 1))
                gwin_ref[:, at + chan : at + chan + 128] = jnp.where(
                    low, pltpu.roll(even, share, 1), odd
                )
    for copy in started:
        copy.wait_send()


def fused(frames, segment_ids, out_grad, ln_gain, w_in, dw_kernel, bn_gain, bn_bias, w_out):
    block, width = frames.shape
    share = w_in.shape[0]
    group = block * TEAM
    chan = width // TEAM
    me = lax.axis_index("seq")
    z, g = me // TEAM, me % TEAM
    ids = jnp.broadcast_to(segment_ids.astype(F32)[:, None], (block, 128))
    lane_half = jnp.arange(128) // share

    def halves(rows_, odd):
        both = jnp.concatenate([rows_, rows_], axis=1)
        return jnp.where(lane_half[None, :] == odd, both, 0.0)

    gain = halves(jnp.broadcast_to(ln_gain[None, :], (8, share)), g % 2)
    prm = halves(
        jnp.concatenate(
            [dw_kernel, bn_gain[None], bn_bias[None], jnp.zeros((7, share), F32)], axis=0
        ),
        z % 2,
    )
    win = (
        w_in.reshape(share, 2, 2, 2, TEAM, share)
        .transpose(4, 0, 2, 1, 3, 5)
        .reshape(TEAM, share, 2 * chan)
    )
    vmem = pl.BlockSpec(memory_space=pltpu.VMEM)
    shape = jax.ShapeDtypeStruct
    ext = group + 2 * PAD
    out, gframes, gwin, gwout, gk, ggain, gbn = pl.pallas_call(
        fused_kernel,
        out_shape=[
            shape((block, width), BF16),
            shape((block, width), BF16),
            shape((share, 2 * width), F32),
            shape((share, width), F32),
            shape((32, 128), F32),
            shape((8, 128), F32),
            shape((2, 8, chan), F32),
        ],
        in_specs=[vmem] * 7,
        out_specs=[vmem] * 7,
        scratch_shapes=[
            pltpu.VMEM((group, width), BF16),
            pltpu.VMEM((ext, 128), F32),
            pltpu.VMEM((group, width), BF16),
            pltpu.VMEM((TEAM * LINE, 8, 128), F32),
            pltpu.VMEM((8, width), F32),
            pltpu.VMEM((width, 2 * chan), BF16),
            pltpu.VMEM((LINE, 40, 128), F32),
            pltpu.VMEM((40, chan), F32),
            pltpu.VMEM((chan, width), BF16),
            pltpu.VMEM((group, width), F32),
            pltpu.VMEM((group, 128), F32),
            pltpu.VMEM((group, width), BF16),
            pltpu.VMEM((group, chan), F32),
            pltpu.VMEM((group, chan), F32),
            pltpu.VMEM((2, ext, 128), F32),
            pltpu.VMEM((group, chan), F32),
            pltpu.VMEM((group, chan), F32),
            pltpu.VMEM((group, chan), BF16),
            pltpu.VMEM((LINE, 2, 8, chan), F32),
            pltpu.VMEM((LINE, 2, 8, chan), F32),
            pltpu.VMEM((2, ext, 128), F32),
            pltpu.VMEM((group, 2 * chan), BF16),
            pltpu.VMEM((2, 2, PAD, chan), F32),
            pltpu.VMEM((2, 2, PAD, chan), F32),
            pltpu.VMEM((32, 8, chan), F32),
            pltpu.VMEM((2, 32, 128), F32),
            pltpu.VMEM((LINE, 32, 128), F32),
            pltpu.VMEM((TEAM, block, width), BF16),
            pltpu.VMEM((TEAM, block, width), BF16),
            pltpu.VMEM((LINE, share, width), BF16),
            pltpu.VMEM((LINE, share, width), BF16),
            pltpu.VMEM((2, LINE, chan, chan), BF16),
            pltpu.VMEM((2, LINE, chan, chan), BF16),
            pltpu.VMEM((2, TEAM, share, chan), BF16),
            pltpu.VMEM((2, TEAM, share, chan), BF16),
            pltpu.VMEM((TEAM, block, width), BF16),
            pltpu.VMEM((TEAM, block, width), BF16),
            pltpu.VMEM((LINE, 8, chan), F32),
            pltpu.VMEM((LINE, 8, chan), F32),
            pltpu.VMEM((2, 8, 128), F32),
            pltpu.VMEM((TEAM, 8, 128), F32),
            pltpu.SemaphoreType.DMA((STAGES, 4)),
            pltpu.SemaphoreType.DMA((STAGES, 4)),
        ],
        compiler_params=pltpu.CompilerParams(
            collective_id=0, has_side_effects=True, vmem_limit_bytes=48 * 1024 * 1024
        ),
    )(frames, ids, out_grad, gain, win, prm, w_out)
    gk = jnp.where(z % 2 == 0, gk[:31, :share], gk[:31, share:])
    ggain = jnp.where(g % 2 == 0, ggain[0, :share], ggain[0, share:])
    gbn = lax.dynamic_slice_in_dim(gbn[:, 0, :], z * share, share, 1)
    return out, gframes, gwin, gwout, gk, ggain, gbn[0], gbn[1]


def solution(mesh):
    small = mesh.shape["seq"] == TEAM * LINE
    return jax.shard_map(
        fused if small else local,
        mesh=mesh,
        in_specs=(
            P(("mix", "seq"), None),
            P(("mix", "seq")),
            P(("mix", "seq"), None),
            P(("mix", "seq")),
            P(("mix", "seq"), None),
            P("mix", "seq"),
            P(("mix", "seq")),
            P(("mix", "seq")),
            P(("mix", "seq"), None),
        ),
        out_specs=(
            P(("mix", "seq"), None),
            P(("mix", "seq"), None),
            P(("mix", "seq"), None),
            P(("mix", "seq"), None),
            P("mix", "seq"),
            P(("mix", "seq")),
            P(("mix", "seq")),
            P(("mix", "seq")),
        ),
        check_vma=False,
    )
```
